256 devices in a mesh: grid: 32 (over x, y, z_lo), orb: 8 (over z_hi, core).
Axes of the slice: x: 4, y: 4, z: 8 (z_hi: 4, z_lo: 2; z = z_hi * 2 + z_lo), core: 2. Of those that a mesh axis runs over, the one named last changes fastest.
Arguments:
- orbitals: float32 [512, 128, 8, 128], P('orb', 'grid'), may hold values from -13 to 13, as said below
- potential: float32 [128, 8, 128], P('grid'), may hold values from -1 to 1
Outputs:
- orthonormal: float32 [512, 128, 8, 128], P('orb', 'grid')
The draws below stay inside these ranges and needn't reach their ends.
Inputs may be any that keep to these rules, and one draw needn't show every extreme that they name: Trial orbitals, real-valued.
All inputs are finite; a program needn't handle non-finite values.
Results may differ from the reference program's by a relative error of at most 0.0003.
Values sent between devices are 32-bit elements; how exact they have to be, the bound alone decides.
A program may use at most 64 MiB of HBM per device.

```python
import math
import jax
import jax.numpy as jnp
from jax import lax

NORB = 512
NY = 8
NZ = 128
NX = 128


def draw_orbitals(key, part):
    keys = jax.random.split(jax.random.fold_in(key, 17), 3)
    orb_scale = jnp.exp(jax.random.uniform(keys[1], (NORB, 1, 1, 1), jnp.float32, math.log(0.1), 0.0))
    ramp = jnp.arange(NX, dtype=jnp.float32) / float(max(NX - 1, 1))
    jitter = jax.random.uniform(keys[2], (NX,), jnp.float32, math.log(0.5), 0.0)
    plane = jnp.exp(math.log(3.0) * ramp + jitter)
    base = jnp.clip(jax.random.normal(keys[0], (NORB, NX, NY, NZ), jnp.float32), -4.0, 4.0)
    return (base * orb_scale * plane[None, :, None, None]).astype(jnp.float32)


def level_of(rng, shape, cuts, smallest, top_value):
    factor_of, own = 1.0, jax.random.fold_in(rng, 6)
    for axis_at, blocks in cuts:
        steps = jnp.exp(jax.random.uniform(jax.random.fold_in(own, axis_at), (blocks,), jnp.float32, smallest / len(cuts), top_value / len(cuts)))
        factor_of = factor_of * jnp.repeat(steps, shape[axis_at] // blocks).reshape([-1 if axis == axis_at else 1 for axis in range(len(shape))])
    return factor_of


def setup_inputs(seed: int = 0) -> dict:
    key_of = jax.random.split(jax.random.key(seed), 3)
    return {
        "orbitals": draw_orbitals(jax.random.fold_in(key_of[2], 71), 0),
        "potential": jnp.clip(jax.random.uniform(key_of[1], (NX, NY, NZ), jnp.float32, -1.0, 1.0) * level_of(key_of[1], (NX, NY, NZ), ((0, 32),), -0.4, 0.0), -1.0, 1.0),
    }


lap_weights = (-205.0 / 72.0, 8.0 / 5.0, -1.0 / 5.0, 8.0 / 315.0, -1.0 / 560.0)
lower_edge = 3.0
upper_edge = 11.0

def wrap_pad(field, axis_num):
    length = field.shape[axis_num]
    head = lax.slice_in_dim(field, length - 4, length, axis=axis_num)
    tail = lax.slice_in_dim(field, 0, 4, axis=axis_num)
    return jnp.concatenate([head, field, tail], axis=axis_num)

def operate(field, potential):
    planes = field.shape[1]
    rows_y = field.shape[2]
    cols_z = field.shape[3]
    padded_x = wrap_pad(field, 1)
    padded_yz = wrap_pad(wrap_pad(field, 2), 3)
    laplace = 3.0 * lap_weights[0] * field
    for offset in range(1, 5):
        weight = lap_weights[offset]
        along_x = padded_x[:, 4 + offset:4 + offset + planes] + padded_x[:, 4 - offset:4 - offset + planes]
        along_y = padded_yz[:, :, 4 + offset:4 + offset + rows_y, 4:4 + cols_z] + padded_yz[:, :, 4 - offset:4 - offset + rows_y, 4:4 + cols_z]
        along_z = padded_yz[:, :, 4:4 + rows_y, 4 + offset:4 + offset + cols_z] + padded_yz[:, :, 4:4 + rows_y, 4 - offset:4 - offset + cols_z]
        laplace = laplace + weight * (along_x + along_y + along_z)
    return potential[None] * field - 0.5 * laplace

def chebyshev(orbital_block, potential):
    center = 0.5 * (upper_edge + lower_edge)
    half_width = 0.5 * (upper_edge - lower_edge)
    prev_field = orbital_block
    this_field = (operate(orbital_block, potential) - center * orbital_block) / half_width
    for degree in range(2):
        next_field = 2.0 * (operate(this_field, potential) - center * this_field) / half_width - prev_field
        prev_field, this_field = (this_field, next_field)
    return this_field

def reference(orbitals, potential):
    grouped = orbitals.reshape(8, NORB // 8, NX, NY, NZ)

    def filter_group(orbital_block):
        return chebyshev(orbital_block, potential)
    filtered = lax.map(filter_group, grouped).reshape(NORB, NX * NY * NZ)
    contract = (((1,), (1,)), ((), ()))
    margin = lax.dot_general(filtered, filtered, contract, precision=lax.Precision.HIGHEST) / float(NX * NY * NZ)
    factor = jnp.linalg.cholesky(margin)
    identity = jnp.eye(NORB, dtype=jnp.float32)
    inverse = jax.scipy.linalg.solve_triangular(factor, identity, lower=True)
    rotated = jnp.dot(inverse, filtered, precision=lax.Precision.HIGHEST)
    return rotated.reshape(NORB, NX, NY, NZ)
```

```python
import functools
import jax, jax.numpy as jnp
from jax import lax
from jax.sharding import PartitionSpec as P
from jax.experimental import pallas as pl
from jax.experimental.pallas import tpu as pltpu
HI = lax.Precision.HIGHEST
NT = (((1,), (1,)), ((), ()))
NN = (((1,), (0,)), ((), ()))

def dot(a, b, dims):
    return lax.dot_general(a, b, dims, precision=HI, preferred_element_type=jnp.float32)

def row_of(block, j):
    return jnp.broadcast_to(block[j:j + 1, :], (8, 128))

def recip(d):
    r = pl.reciprocal(d, approx=True)
    r = r * (2.0 - d * r)
    return r * (2.0 - d * r)

def factor_block(s_ref, w_ref, base):
    sub = lax.broadcasted_iota(jnp.int32, (8, 128), 0)
    lane = lax.broadcasted_iota(jnp.int32, (8, 128), 1)
    s = [s_ref[pl.ds(base + 8 * i, 8), :] for i in range(16)]
    w = [jnp.where(lane == sub + 8 * i, 1.0, 0.0).astype(jnp.float32) for i in range(16)]
    for p in range(16):
        col = [jnp.broadcast_to(s[p][:, 8 * p + j:8 * p + j + 1], (8, 128)) for j in range(8)]
        fac, rinv, s_rows, w_rows = {}, [], [], []
        sp, wp = s[p], w[p]
        dvec = jnp.ones((8, 128), jnp.float32)
        for j in range(8):
            d = row_of(col[j], j)
            r = recip(d)
            rinv.append(r)
            dvec = jnp.where(sub == j, d, dvec)
            m = jnp.where(sub > j, col[j] * r, 0.0)
            for k in range(j + 1, 8):
                fac[j, k] = row_of(col[k], j)
                col[k] = col[k] - m * fac[j, k]
            s_rows.append(row_of(sp, j))
            w_rows.append(row_of(wp, j))
            if j < 7:
                sp = sp - m * s_rows[j]
                wp = wp - m * w_rows[j]
        w[p] = wp * lax.rsqrt(dvec)
        for i in range(p + 1, 16):
            raw = [jnp.broadcast_to(s[i][:, 8 * p + j:8 * p + j + 1], (8, 128)) for j in range(8)]
            si, wi = s[i], w[i]
            for j in range(8):
                m = raw[j] * rinv[j]
                for k in range(j + 1, 8):
                    raw[k] = raw[k] - m * fac[j, k]
                si = si - m * s_rows[j]
                wi = wi - m * w_rows[j]
            s[i], w[i] = si, wi
    for i in range(16):
        w_ref[8 * i:8 * i + 8, :] = w[i]

def blk(i, j):
    return i * (i + 1) // 2 + j

def rotate_kernel(cells, g_ref, f_ref, y_ref, a_ref, x_ref, w_ref):
    a_ref[...] = g_ref[...] * (1.0 / cells)
    for q in range(4):
        x_ref[:, 128 * q:128 * q + 128] = f_ref[:, q, :]
    for b in range(4):
        factor_block(a_ref, w_ref, 128 * blk(b, b))
        w = w_ref[...]
        low = {}
        for i in range(b + 1, 4):
            low[i] = dot(a_ref[pl.ds(128 * blk(i, b), 128), :], w, NT)
            for j in range(b + 1, i + 1):
                rows = pl.ds(128 * blk(i, j), 128)
                a_ref[rows, :] = a_ref[rows, :] - dot(low[i], low[j], NT)
        y = dot(w, x_ref[128 * b:128 * b + 128, :], NN)
        for q in range(4):
            y_ref[128 * b:128 * b + 128, q, :] = y[:, 128 * q:128 * q + 128]
        for i in range(b + 1, 4):
            rows = slice(128 * i, 128 * i + 128)
            x_ref[rows, :] = x_ref[rows, :] - dot(low[i], y, NN)

def rotate(g, f, cells):
    vm = pl.BlockSpec(memory_space=pltpu.VMEM)
    return pl.pallas_call(functools.partial(rotate_kernel, cells),
        out_shape=jax.ShapeDtypeStruct((512, 4, 128), jnp.float32),
        in_specs=[vm, vm], out_specs=vm,
        scratch_shapes=[pltpu.VMEM((1280, 128), jnp.float32), pltpu.VMEM((512, 512), jnp.float32), pltpu.VMEM((128, 128), jnp.float32)],
        compiler_params=pltpu.CompilerParams(vmem_limit_bytes=32 << 20))(g, f)

def margin_kernel(f_ref, g_ref, x_ref):
    for q in range(4):
        x_ref[:, 128 * q:128 * q + 128] = f_ref[:, q, :]
    for i in range(4):
        xi = x_ref[128 * i:128 * i + 128, :]
        for j in range(i + 1):
            g_ref[pl.ds(128 * blk(i, j), 128), :] = dot(xi, x_ref[128 * j:128 * j + 128, :], NT)

def margin_part(f):
    vm = pl.BlockSpec(memory_space=pltpu.VMEM)
    return pl.pallas_call(margin_kernel, out_shape=jax.ShapeDtypeStruct((1280, 128), jnp.float32),
        in_specs=[vm], out_specs=vm, scratch_shapes=[pltpu.VMEM((512, 512), jnp.float32)],
        compiler_params=pltpu.CompilerParams(vmem_limit_bytes=32 << 20))(f)

W = (-205.0 / 72.0, 8.0 / 5.0, -1.0 / 5.0, 8.0 / 315.0, -1.0 / 560.0)

def filter_kernel(v_ref, p_ref, o_ref, a_ref, b_ref):
    step = 4
    def fill(ref):
        ref[:, 0:4] = ref[:, 128:132]
        ref[:, 132:136] = ref[:, 4:8]
    def level(src, prev, dst, gain):
        scale = -0.5 * gain
        w = [scale * c for c in W]
        def body(t, carry):
            base = t * step
            pot = p_ref[pl.ds(base, step)]
            diag = gain * (pot - 7.0) + 3.0 * w[0]
            for o in range(2):
                win = src[o, pl.ds(base, step + 8)]
                v = win[4:4 + step]
                acc = diag * v
                u1 = pltpu.roll(v, 1, 1) + pltpu.roll(v, 7, 1)
                r4 = pltpu.roll(v, 4, 1)
                u2 = pltpu.roll(v + r4, 2, 1)
                u3 = pltpu.roll(u1, 4, 1)
                side = [u1, u2, u3, r4 + r4]
                for m in range(1, 5):
                    zz = pltpu.roll(v, m, 2) + pltpu.roll(v, 128 - m, 2)
                    xx = win[4 + m:4 + m + step] + win[4 - m:4 - m + step]
                    acc = acc + w[m] * (side[m - 1] + zz + xx)
                if prev is not None:
                    acc = acc - prev(o, base)
                dst(o, base, acc)
            return carry
        lax.fori_loop(0, 128 // step, body, 0)
    a_ref[:, 4:132] = v_ref[...]
    fill(a_ref)
    def into(ref, off):
        def put(o, base, val):
            ref[o, pl.ds(base + off, step)] = val
        return put
    def of(ref, off):
        return lambda o, base: ref[o, pl.ds(base + off, step)]
    level(a_ref, None, into(b_ref, 4), 0.25)
    fill(b_ref)
    level(b_ref, of(a_ref, 4), into(a_ref, 4), 0.5)
    fill(a_ref)
    level(a_ref, of(b_ref, 4), into(o_ref, 0), 0.5)

def filt(v, p):
    vm = pl.BlockSpec(memory_space=pltpu.VMEM)
    return pl.pallas_call(filter_kernel, out_shape=jax.ShapeDtypeStruct(v.shape, jnp.float32),
        in_specs=[vm, vm], out_specs=vm,
        scratch_shapes=[pltpu.VMEM((2, 136, 8, 128), jnp.float32)] * 2,
        compiler_params=pltpu.CompilerParams(vmem_limit_bytes=32 << 20))(v, p)

MESH = pl.DeviceIdType.MESH


def any_spec():
    return pl.BlockSpec(memory_space=pl.ANY)


def spread_kernel(orb_ref, pot_ref, v_ref, p_ref, send, recv, psend, precv, own):
    me, my_orb = lax.axis_index("grid"), lax.axis_index("orb")
    bar = pltpu.get_barrier_semaphore()

    def greet(d, carry):
        pl.semaphore_signal(bar, inc=1, device_id=(lax.rem(me + d, 32), my_orb), device_id_type=MESH)
        return carry

    lax.fori_loop(1, 32, greet, 0)
    pl.semaphore_wait(bar, 31)

    def copies(d):
        to = lax.rem(me + d, 32)
        field = pltpu.make_async_remote_copy(
            src_ref=orb_ref.at[pl.ds(2 * to, 2)],
            dst_ref=v_ref.at[:, pl.ds(4 * me, 4)],
            send_sem=send.at[d], recv_sem=recv.at[d],
            device_id=(to, my_orb), device_id_type=MESH)
        pot = pltpu.make_async_remote_copy(
            src_ref=pot_ref, dst_ref=p_ref.at[pl.ds(4 * me, 4)],
            send_sem=psend.at[d], recv_sem=precv.at[d],
            device_id=(to, my_orb), device_id_type=MESH)
        return field, pot

    def start(d, carry):
        for c in copies(d):
            c.start()
        return carry

    lax.fori_loop(1, 32, start, 0)
    mine = pltpu.make_async_copy(orb_ref.at[pl.ds(2 * me, 2)], v_ref.at[:, pl.ds(4 * me, 4)], own.at[0])
    mine.start()
    minep = pltpu.make_async_copy(pot_ref, p_ref.at[pl.ds(4 * me, 4)], own.at[1])
    minep.start()
    mine.wait()
    minep.wait()

    def finish(d, carry):
        for c in copies(d):
            c.wait()
        return carry

    lax.fori_loop(1, 32, finish, 0)


def spread(orbitals, potential):
    dma = pltpu.SemaphoreType.DMA
    return pl.pallas_call(
        spread_kernel,
        out_shape=(jax.ShapeDtypeStruct((2, 128, 8, 128), jnp.float32),
                   jax.ShapeDtypeStruct((128, 8, 128), jnp.float32)),
        in_specs=[any_spec()] * 2, out_specs=(any_spec(),) * 2,
        scratch_shapes=[dma((32,))] * 4 + [dma((2,))],
        compiler_params=pltpu.CompilerParams(collective_id=1, has_side_effects=True),
    )(orbitals, potential)


def collect_kernel(f_ref, m_ref, slab, send, recv, send2, recv2, own):
    me, my_orb = lax.axis_index("grid"), lax.axis_index("orb")
    bar = pltpu.get_barrier_semaphore()

    def greet(d, carry):
        pl.semaphore_signal(bar, inc=1, device_id=(lax.rem(me + d, 32), my_orb), device_id_type=MESH)
        return carry

    def greet_orb(d, carry):
        pl.semaphore_signal(bar, inc=1, device_id=(me, lax.rem(my_orb + d, 8)), device_id_type=MESH)
        return carry

    lax.fori_loop(1, 32, greet, 0)
    lax.fori_loop(1, 8, greet_orb, 0)
    pl.semaphore_wait(bar, 38)

    def piece(d):
        to = lax.rem(me + d, 32)
        return pltpu.make_async_remote_copy(
            src_ref=f_ref.at[:, pl.ds(4 * to, 4)],
            dst_ref=slab.at[pl.ds(2 * me, 2)],
            send_sem=send.at[d], recv_sem=recv.at[d],
            device_id=(to, my_orb), device_id_type=MESH)

    def start(d, carry):
        piece(d).start()
        return carry

    lax.fori_loop(1, 32, start, 0)
    mine = pltpu.make_async_copy(f_ref.at[:, pl.ds(4 * me, 4)], slab.at[pl.ds(2 * me, 2)], own.at[0])
    mine.start()
    mine.wait()

    def finish(d, carry):
        piece(d).wait()
        return carry

    lax.fori_loop(1, 32, finish, 0)

    def cells(d):
        to = lax.rem(my_orb + d, 8)
        return pltpu.make_async_remote_copy(
            src_ref=slab.at[:, to // 2, lax.rem(to, 2)],
            dst_ref=m_ref.at[pl.ds(64 * my_orb, 64)],
            send_sem=send2.at[d], recv_sem=recv2.at[d],
            device_id=(me, to), device_id_type=MESH)

    for d in range(1, 8):
        cells(d).start()
    mine = pltpu.make_async_copy(slab.at[:, my_orb // 2, lax.rem(my_orb, 2)], m_ref.at[pl.ds(64 * my_orb, 64)], own.at[1])
    mine.start()
    mine.wait()
    for d in range(1, 8):
        cells(d).wait()


def collect(f):
    dma = pltpu.SemaphoreType.DMA
    return pl.pallas_call(
        collect_kernel,
        out_shape=jax.ShapeDtypeStruct((512, 4, 128), jnp.float32),
        in_specs=[any_spec()], out_specs=any_spec(),
        scratch_shapes=[pltpu.VMEM((64, 4, 2, 4, 128), jnp.float32), dma((32,)), dma((32,)), dma((8,)), dma((8,)), dma((2,))],
        compiler_params=pltpu.CompilerParams(collective_id=2, has_side_effects=True, vmem_limit_bytes=32 << 20),
    )(f)


def reduce_kernel(g_ref, out_ref, parts, zparts, send, recv, zsend, zrecv, asend, arecv, own):
    me, my_orb = lax.axis_index("grid"), lax.axis_index("orb")
    z_lo, z_hi = lax.rem(me, 2), my_orb // 2
    at = (me // 2) * 2 + lax.rem(my_orb, 2)
    zat = z_hi * 2 + z_lo

    def plane(i):
        return (i // 2) * 2 + z_lo, z_hi * 2 + lax.rem(i, 2)

    def column(z):
        return (me // 2) * 2 + lax.rem(z, 2), (z // 2) * 2 + lax.rem(my_orb, 2)

    bar = pltpu.get_barrier_semaphore()

    def greet(d, carry):
        pl.semaphore_signal(bar, inc=1, device_id=plane(lax.rem(at + d, 32)), device_id_type=MESH)
        return carry

    def greet_z(d, carry):
        pl.semaphore_signal(bar, inc=1, device_id=column(lax.rem(zat + d, 8)), device_id_type=MESH)
        return carry

    lax.fori_loop(1, 32, greet, 0)
    lax.fori_loop(1, 8, greet_z, 0)
    pl.semaphore_wait(bar, 38)

    def scatter(d):
        to = lax.rem(at + d, 32)
        return pltpu.make_async_remote_copy(
            src_ref=g_ref.at[pl.ds(pl.multiple_of(40 * to, 8), 40)], dst_ref=parts.at[at],
            send_sem=send.at[d], recv_sem=recv.at[d],
            device_id=plane(to), device_id_type=MESH)

    def start(d, carry):
        scatter(d).start()
        return carry

    lax.fori_loop(1, 32, start, 0)
    my_rows = pl.ds(pl.multiple_of(40 * at, 8), 40)
    parts[at] = g_ref[my_rows, :]

    def finish(d, carry):
        scatter(d).wait()
        return carry

    lax.fori_loop(1, 32, finish, 0)

    def add(i, total):
        return total + parts[i]

    zparts[zat] = lax.fori_loop(1, 32, add, parts[0])

    def exchange(d):
        return pltpu.make_async_remote_copy(
            src_ref=zparts.at[zat], dst_ref=zparts.at[zat],
            send_sem=zsend.at[d], recv_sem=zrecv.at[d],
            device_id=column(lax.rem(zat + d, 8)), device_id_type=MESH)

    for d in range(1, 8):
        exchange(d).start()
    for d in range(1, 8):
        exchange(d).wait()
    total = zparts[0]
    for z in range(1, 8):
        total = total + zparts[z]
    out_ref[my_rows, :] = total

    def gather(d):
        return pltpu.make_async_remote_copy(
            src_ref=out_ref.at[my_rows], dst_ref=out_ref.at[my_rows],
            send_sem=asend.at[d], recv_sem=arecv.at[d],
            device_id=plane(lax.rem(at + d, 32)), device_id_type=MESH)

    def start3(d, carry):
        gather(d).start()
        return carry

    def finish3(d, carry):
        gather(d).wait()
        return carry

    lax.fori_loop(1, 32, start3, 0)
    lax.fori_loop(1, 32, finish3, 0)


def reduce_all(g):
    dma = pltpu.SemaphoreType.DMA
    vm = pl.BlockSpec(memory_space=pltpu.VMEM)
    return pl.pallas_call(
        reduce_kernel,
        out_shape=jax.ShapeDtypeStruct((1280, 128), jnp.float32),
        in_specs=[vm], out_specs=vm,
        scratch_shapes=[pltpu.VMEM((32, 40, 128), jnp.float32), pltpu.VMEM((8, 40, 128), jnp.float32),
                        dma((32,)), dma((32,)), dma((8,)), dma((8,)), dma((32,)), dma((32,)), dma((2,))],
        compiler_params=pltpu.CompilerParams(collective_id=3, has_side_effects=True, vmem_limit_bytes=32 << 20),
    )(g)


def deliver_kernel(y_ref, out_ref, send, recv, own):
    me, my_orb = lax.axis_index("grid"), lax.axis_index("orb")
    bar = pltpu.get_barrier_semaphore()
    for d in range(1, 8):
        pl.semaphore_signal(bar, inc=1, device_id=(me, lax.rem(my_orb + d, 8)), device_id_type=MESH)
    pl.semaphore_wait(bar, 7)

    def rows(d):
        to = lax.rem(my_orb + d, 8)
        return pltpu.make_async_remote_copy(
            src_ref=y_ref.at[pl.ds(64 * to, 64)],
            dst_ref=out_ref.at[:, my_orb // 2, lax.rem(my_orb, 2)],
            send_sem=send.at[d], recv_sem=recv.at[d],
            device_id=(me, to), device_id_type=MESH)

    for d in range(1, 8):
        rows(d).start()
    mine = pltpu.make_async_copy(y_ref.at[pl.ds(64 * my_orb, 64)], out_ref.at[:, my_orb // 2, lax.rem(my_orb, 2)], own.at[0])
    mine.start()
    mine.wait()
    for d in range(1, 8):
        rows(d).wait()


def deliver(y):
    dma = pltpu.SemaphoreType.DMA
    return pl.pallas_call(
        deliver_kernel,
        out_shape=jax.ShapeDtypeStruct((64, 4, 2, 4, 128), jnp.float32),
        in_specs=[any_spec()], out_specs=any_spec(),
        scratch_shapes=[dma((8,)), dma((8,)), dma((1,))],
        compiler_params=pltpu.CompilerParams(collective_id=4, has_side_effects=True),
    )(y)


def per_device(orbitals, potential):
    field, pot = spread(orbitals, potential)
    filtered = filt(field, pot)
    cells = collect(filtered.reshape(2, 128, 2, 4, 128))
    margin = reduce_all(margin_part(cells))
    rotated = rotate(margin, cells, 131072.0)
    return deliver(rotated).reshape(64, 4, 8, 128)


def solution(mesh):
    in_specs = (P("orb", "grid", None, None), P("grid", None, None))
    out_specs = P("orb", "grid", None, None)
    return jax.shard_map(
        per_device, mesh=mesh, in_specs=in_specs, out_specs=out_specs, check_vma=False
    )
```

```python
import functools
import jax, jax.numpy as jnp
from jax import lax
from jax.sharding import PartitionSpec as P
from jax.experimental import pallas as pl
from jax.experimental.pallas import tpu as pltpu
HI = lax.Precision.HIGHEST
NT = (((1,), (1,)), ((), ()))
NN = (((1,), (0,)), ((), ()))

def dot(a, b, dims):
    return lax.dot_general(a, b, dims, precision=HI, preferred_element_type=jnp.float32)

def row_of(block, j):
    return jnp.broadcast_to(block[j:j + 1, :], (8, 128))

def recip(d):
    r = pl.reciprocal(d, approx=True)
    r = r * (2.0 - d * r)
    return r * (2.0 - d * r)

def factor_block(s_ref, w_ref, base):
    sub = lax.broadcasted_iota(jnp.int32, (8, 128), 0)
    lane = lax.broadcasted_iota(jnp.int32, (8, 128), 1)
    s = [s_ref[pl.ds(base + 8 * i, 8), :] for i in range(16)]
    w = [jnp.where(lane == sub + 8 * i, 1.0, 0.0).astype(jnp.float32) for i in range(16)]
    for p in range(16):
        col = [jnp.broadcast_to(s[p][:, 8 * p + j:8 * p + j + 1], (8, 128)) for j in range(8)]
        fac, rinv, s_rows, w_rows = {}, [], [], []
        sp, wp = s[p], w[p]
        dvec = jnp.ones((8, 128), jnp.float32)
        for j in range(8):
            d = row_of(col[j], j)
            r = recip(d)
            rinv.append(r)
            dvec = jnp.where(sub == j, d, dvec)
            m = jnp.where(sub > j, col[j] * r, 0.0)
            for k in range(j + 1, 8):
                fac[j, k] = row_of(col[k], j)
                col[k] = col[k] - m * fac[j, k]
            s_rows.append(row_of(sp, j))
            w_rows.append(row_of(wp, j))
            if j < 7:
                sp = sp - m * s_rows[j]
                wp = wp - m * w_rows[j]
        w[p] = wp * lax.rsqrt(dvec)
        for i in range(p + 1, 16):
            raw = [jnp.broadcast_to(s[i][:, 8 * p + j:8 * p + j + 1], (8, 128)) for j in range(8)]
            si, wi = s[i], w[i]
            for j in range(8):
                m = raw[j] * rinv[j]
                for k in range(j + 1, 8):
                    raw[k] = raw[k] - m * fac[j, k]
                si = si - m * s_rows[j]
                wi = wi - m * w_rows[j]
            s[i], w[i] = si, wi
    for i in range(16):
        w_ref[8 * i:8 * i + 8, :] = w[i]

def blk(i, j):
    return i * (i + 1) // 2 + j

def rotate_kernel(cells, g_ref, f_ref, y_ref, a_ref, x_ref, w_ref):
    a_ref[...] = g_ref[...] * (1.0 / cells)
    for q in range(4):
        x_ref[:, 128 * q:128 * q + 128] = f_ref[:, q, :]
    for b in range(4):
        factor_block(a_ref, w_ref, 128 * blk(b, b))
        w = w_ref[...]
        low = {}
        for i in range(b + 1, 4):
            low[i] = dot(a_ref[pl.ds(128 * blk(i, b), 128), :], w, NT)
            for j in range(b + 1, i + 1):
                rows = pl.ds(128 * blk(i, j), 128)
                a_ref[rows, :] = a_ref[rows, :] - dot(low[i], low[j], NT)
        y = dot(w, x_ref[128 * b:128 * b + 128, :], NN)
        for q in range(4):
            y_ref[128 * b:128 * b + 128, q, :] = y[:, 128 * q:128 * q + 128]
        for i in range(b + 1, 4):
            rows = slice(128 * i, 128 * i + 128)
            x_ref[rows, :] = x_ref[rows, :] - dot(low[i], y, NN)

def rotate(g, f, cells):
    vm = pl.BlockSpec(memory_space=pltpu.VMEM)
    return pl.pallas_call(functools.partial(rotate_kernel, cells),
        out_shape=jax.ShapeDtypeStruct((512, 4, 128), jnp.float32),
        in_specs=[vm, vm], out_specs=vm,
        scratch_shapes=[pltpu.VMEM((1280, 128), jnp.float32), pltpu.VMEM((512, 512), jnp.float32), pltpu.VMEM((128, 128), jnp.float32)],
        compiler_params=pltpu.CompilerParams(vmem_limit_bytes=32 << 20))(g, f)

def margin_kernel(f_ref, g_ref, x_ref):
    for q in range(4):
        x_ref[:, 128 * q:128 * q + 128] = f_ref[:, q, :]
    for i in range(4):
        xi = x_ref[128 * i:128 * i + 128, :]
        for j in range(i + 1):
            g_ref[pl.ds(128 * blk(i, j), 128), :] = dot(xi, x_ref[128 * j:128 * j + 128, :], NT)

def margin_part(f):
    vm = pl.BlockSpec(memory_space=pltpu.VMEM)
    return pl.pallas_call(margin_kernel, out_shape=jax.ShapeDtypeStruct((1280, 128), jnp.float32),
        in_specs=[vm], out_specs=vm, scratch_shapes=[pltpu.VMEM((512, 512), jnp.float32)],
        compiler_params=pltpu.CompilerParams(vmem_limit_bytes=32 << 20))(f)

W = (-205.0 / 72.0, 8.0 / 5.0, -1.0 / 5.0, 8.0 / 315.0, -1.0 / 560.0)

MESH = pl.DeviceIdType.MESH


def any_spec():
    return pl.BlockSpec(memory_space=pl.ANY)


STEP = 64


def shift_matrix():
    i = lax.broadcasted_iota(jnp.int32, (128, 128), 0)
    j = lax.broadcasted_iota(jnp.int32, (128, 128), 1)
    apart = jnp.abs(i - j)
    apart = jnp.minimum(apart, 128 - apart)
    out = jnp.zeros((128, 128), jnp.float32)
    for m in range(1, 5):
        out = jnp.where(apart == m, W[m], out)
    return out


def apply_level(src, pot_ref, along_z, gain, prev, put):
    w = [-0.5 * gain * c for c in W]
    shifts = along_z * (-0.5 * gain)

    def body(t, carry):
        base = t * STEP
        win = src[pl.ds(base, STEP + 8)]
        v = win[4:4 + STEP]
        acc = (gain * (pot_ref[pl.ds(base, STEP)] - 7.0) + 3.0 * w[0]) * v
        acc = acc + dot(v.reshape(STEP * 8, 128), shifts, NN).reshape(STEP, 8, 128)
        u1 = pltpu.roll(v, 1, 1) + pltpu.roll(v, 7, 1)
        r4 = pltpu.roll(v, 4, 1)
        side = [u1, pltpu.roll(v + r4, 2, 1), pltpu.roll(u1, 4, 1), r4 + r4]
        for m in range(1, 5):
            xx = win[4 + m:4 + m + STEP] + win[4 - m:4 - m + STEP]
            acc = acc + w[m] * (side[m - 1] + xx)
        if prev is not None:
            acc = acc - prev[pl.ds(base + 4, STEP)]
        put(base, acc)
        return carry

    lax.fori_loop(0, 128 // STEP, body, 0)


def fill(ref):
    ref[0:4] = ref[128:132]
    ref[132:136] = ref[4:8]


def front_kernel(orb_ref, pot_ref, m_ref, a, b, pot, c, slab,
                 send, recv, psend, precv, asend, arecv, bsend, brecv, own):
    me, my_orb = lax.axis_index("grid"), lax.axis_index("orb")
    xy, z_lo = me // 2, lax.rem(me, 2)
    z_hi, core = my_orb // 2, lax.rem(my_orb, 2)
    zc = (z_hi * 2 + z_lo) * 2 + core

    def stack(i):
        z, k = i // 2, lax.rem(i, 2)
        lo, hi = lax.rem(z, 2), z // 2
        return (xy * 2 + lo, hi * 2 + k), lo, hi, k

    bar = pltpu.get_barrier_semaphore()

    def greet(d, carry):
        pl.semaphore_signal(bar, inc=1, device_id=(lax.rem(me + d, 32), my_orb), device_id_type=MESH)
        return carry

    def greet_stack(d, carry):
        pl.semaphore_signal(bar, inc=1, device_id=stack(lax.rem(zc + d, 16))[0], device_id_type=MESH)
        return carry

    lax.fori_loop(1, 32, greet, 0)
    lax.fori_loop(1, 16, greet_stack, 0)
    pl.semaphore_wait(bar, 46)

    def orb_copy(k, d):
        to = lax.rem(me + d, 32)
        return pltpu.make_async_remote_copy(
            src_ref=orb_ref.at[2 * to + k], dst_ref=a.at[k, pl.ds(4 + 4 * me, 4)],
            send_sem=send.at[k, d], recv_sem=recv.at[k, d],
            device_id=(to, my_orb), device_id_type=MESH)

    def pot_copy(d):
        return pltpu.make_async_remote_copy(
            src_ref=pot_ref, dst_ref=pot.at[pl.ds(4 * me, 4)],
            send_sem=psend.at[d], recv_sem=precv.at[d],
            device_id=(lax.rem(me + d, 32), my_orb), device_id_type=MESH)

    def plane_copy(k, d):
        to = lax.rem(xy + d, 16)
        return pltpu.make_async_remote_copy(
            src_ref=c.at[k, pl.ds(8 * to, 8)], dst_ref=slab.at[k, xy],
            send_sem=asend.at[k, d], recv_sem=arecv.at[k, d],
            device_id=(to * 2 + z_lo, my_orb), device_id_type=MESH)

    def cell_copy(k, d):
        device, lo, hi, half = stack(lax.rem(zc + d, 16))
        return pltpu.make_async_remote_copy(
            src_ref=slab.at[k, :, 4 * lo + hi, half], dst_ref=m_ref.at[my_orb, :, z_lo, k],
            send_sem=bsend.at[k, d], recv_sem=brecv.at[k, d],
            device_id=device, device_id_type=MESH)

    def each(first, last, do):
        def body(d, carry):
            do(d)
            return carry
        lax.fori_loop(first, last, body, 0)

    def start_first(d):
        orb_copy(0, d).start()
        pot_copy(d).start()

    each(1, 32, start_first)
    each(1, 32, lambda d: orb_copy(1, d).start())
    local = [pltpu.make_async_copy(orb_ref.at[2 * me + k], a.at[k, pl.ds(4 + 4 * me, 4)], own.at[k]) for k in range(2)]
    local.append(pltpu.make_async_copy(pot_ref, pot.at[pl.ds(4 * me, 4)], own.at[2]))
    for copy in local:
        copy.start()
    for copy in local:
        copy.wait()

    def wait_pot(d):
        pot_copy(d).wait()

    each(1, 32, wait_pot)
    along_z = shift_matrix()
    for k in range(2):
        each(1, 32, lambda d: orb_copy(k, d).wait())
        ak, bk, ck = a.at[k], b.at[k], c.at[k]

        def put_b(base, value):
            bk[pl.ds(base + 4, STEP)] = value

        def put_a(base, value):
            ak[pl.ds(base + 4, STEP)] = value

        def put_c(base, value):
            ck[pl.ds(base, STEP), 0] = value[:, 0:4]
            ck[pl.ds(base, STEP), 1] = value[:, 4:8]

        fill(ak)
        apply_level(ak, pot, along_z, 0.25, None, put_b)
        fill(bk)
        apply_level(bk, pot, along_z, 0.5, ak, put_a)
        fill(ak)
        apply_level(ak, pot, along_z, 0.5, bk, put_c)
        each(1, 16, lambda d: plane_copy(k, d).start())
        mine = pltpu.make_async_copy(c.at[k, pl.ds(8 * xy, 8)], slab.at[k, xy], own.at[3 + k])
        mine.start()
        mine.wait()
    for k in range(2):
        each(1, 16, lambda d: plane_copy(k, d).wait())
        each(1, 16, lambda d: cell_copy(k, d).start())
        mine = pltpu.make_async_copy(slab.at[k, :, 4 * z_lo + z_hi, core], m_ref.at[my_orb, :, z_lo, k], own.at[5 + k])
        mine.start()
        mine.wait()
    for k in range(2):
        each(1, 16, lambda d: cell_copy(k, d).wait())


def front(orbitals, potential):
    dma, vmem, f32 = pltpu.SemaphoreType.DMA, pltpu.VMEM, jnp.float32
    return pl.pallas_call(
        front_kernel,
        out_shape=jax.ShapeDtypeStruct((8, 16, 2, 2, 4, 128), f32),
        in_specs=[any_spec()] * 2, out_specs=any_spec(),
        scratch_shapes=[vmem((2, 136, 8, 128), f32), vmem((2, 136, 8, 128), f32), vmem((128, 8, 128), f32),
                        vmem((2, 128, 2, 4, 128), f32), vmem((2, 16, 8, 2, 4, 128), f32),
                        dma((2, 32)), dma((2, 32)), dma((32,)), dma((32,)), dma((2, 16)), dma((2, 16)),
                        dma((2, 16)), dma((2, 16)), dma((7,))],
        compiler_params=pltpu.CompilerParams(collective_id=1, has_side_effects=True, vmem_limit_bytes=60 << 20),
    )(orbitals, potential)


def reduce_kernel(g_ref, out_ref, parts, zparts, send, recv, zsend, zrecv, asend, arecv, own):
    me, my_orb = lax.axis_index("grid"), lax.axis_index("orb")
    z_lo, z_hi = lax.rem(me, 2), my_orb // 2
    at = (me // 2) * 2 + lax.rem(my_orb, 2)
    zat = z_hi * 2 + z_lo

    def plane(i):
        return (i // 2) * 2 + z_lo, z_hi * 2 + lax.rem(i, 2)

    def column(z):
        return (me // 2) * 2 + lax.rem(z, 2), (z // 2) * 2 + lax.rem(my_orb, 2)

    bar = pltpu.get_barrier_semaphore()

    def greet(d, carry):
        pl.semaphore_signal(bar, inc=1, device_id=plane(lax.rem(at + d, 32)), device_id_type=MESH)
        return carry

    def greet_z(d, carry):
        pl.semaphore_signal(bar, inc=1, device_id=column(lax.rem(zat + d, 8)), device_id_type=MESH)
        return carry

    lax.fori_loop(1, 32, greet, 0)
    lax.fori_loop(1, 8, greet_z, 0)
    pl.semaphore_wait(bar, 38)

    def scatter(d):
        to = lax.rem(at + d, 32)
        return pltpu.make_async_remote_copy(
            src_ref=g_ref.at[pl.ds(pl.multiple_of(40 * to, 8), 40)], dst_ref=parts.at[at],
            send_sem=send.at[d], recv_sem=recv.at[d],
            device_id=plane(to), device_id_type=MESH)

    def start(d, carry):
        scatter(d).start()
        return carry

    lax.fori_loop(1, 32, start, 0)
    my_rows = pl.ds(pl.multiple_of(40 * at, 8), 40)
    parts[at] = g_ref[my_rows, :]

    def finish(d, carry):
        scatter(d).wait()
        return carry

    lax.fori_loop(1, 32, finish, 0)

    def add(i, total):
        return total + parts[i]

    zparts[zat] = lax.fori_loop(1, 32, add, parts[0])

    def exchange(d):
        return pltpu.make_async_remote_copy(
            src_ref=zparts.at[zat], dst_ref=zparts.at[zat],
            send_sem=zsend.at[d], recv_sem=zrecv.at[d],
            device_id=column(lax.rem(zat + d, 8)), device_id_type=MESH)

    for d in range(1, 8):
        exchange(d).start()
    for d in range(1, 8):
        exchange(d).wait()
    total = zparts[0]
    for z in range(1, 8):
        total = total + zparts[z]
    out_ref[my_rows, :] = total

    def gather(d):
        return pltpu.make_async_remote_copy(
            src_ref=out_ref.at[my_rows], dst_ref=out_ref.at[my_rows],
            send_sem=asend.at[d], recv_sem=arecv.at[d],
            device_id=plane(lax.rem(at + d, 32)), device_id_type=MESH)

    def start3(d, carry):
        gather(d).start()
        return carry

    def finish3(d, carry):
        gather(d).wait()
        return carry

    lax.fori_loop(1, 32, start3, 0)
    lax.fori_loop(1, 32, finish3, 0)


def reduce_all(g):
    dma = pltpu.SemaphoreType.DMA
    vm = pl.BlockSpec(memory_space=pltpu.VMEM)
    return pl.pallas_call(
        reduce_kernel,
        out_shape=jax.ShapeDtypeStruct((1280, 128), jnp.float32),
        in_specs=[vm], out_specs=vm,
        scratch_shapes=[pltpu.VMEM((32, 40, 128), jnp.float32), pltpu.VMEM((8, 40, 128), jnp.float32),
                        dma((32,)), dma((32,)), dma((8,)), dma((8,)), dma((32,)), dma((32,)), dma((2,))],
        compiler_params=pltpu.CompilerParams(collective_id=3, has_side_effects=True, vmem_limit_bytes=32 << 20),
    )(g)


def deliver_kernel(y_ref, out_ref, send, recv, own):
    me, my_orb = lax.axis_index("grid"), lax.axis_index("orb")
    bar = pltpu.get_barrier_semaphore()
    for d in range(1, 8):
        pl.semaphore_signal(bar, inc=1, device_id=(me, lax.rem(my_orb + d, 8)), device_id_type=MESH)
    pl.semaphore_wait(bar, 7)

    def rows(d):
        to = lax.rem(my_orb + d, 8)
        return pltpu.make_async_remote_copy(
            src_ref=y_ref.at[pl.ds(64 * to, 64)],
            dst_ref=out_ref.at[:, my_orb // 2, lax.rem(my_orb, 2)],
            send_sem=send.at[d], recv_sem=recv.at[d],
            device_id=(me, to), device_id_type=MESH)

    for d in range(1, 8):
        rows(d).start()
    mine = pltpu.make_async_copy(y_ref.at[pl.ds(64 * my_orb, 64)], out_ref.at[:, my_orb // 2, lax.rem(my_orb, 2)], own.at[0])
    mine.start()
    mine.wait()
    for d in range(1, 8):
        rows(d).wait()


def deliver(y):
    dma = pltpu.SemaphoreType.DMA
    return pl.pallas_call(
        deliver_kernel,
        out_shape=jax.ShapeDtypeStruct((64, 4, 2, 4, 128), jnp.float32),
        in_specs=[any_spec()], out_specs=any_spec(),
        scratch_shapes=[dma((8,)), dma((8,)), dma((1,))],
        compiler_params=pltpu.CompilerParams(collective_id=4, has_side_effects=True),
    )(y)


def per_device(orbitals, potential):
    cells = front(orbitals, potential).reshape(512, 4, 128)
    margin = reduce_all(margin_part(cells))
    rotated = rotate(margin, cells, 131072.0)
    return deliver(rotated).reshape(64, 4, 8, 128)


def solution(mesh):
    in_specs = (P("orb", "grid", None, None), P("grid", None, None))
    out_specs = P("orb", "grid", None, None)
    return jax.shard_map(
        per_device, mesh=mesh, in_specs=in_specs, out_specs=out_specs, check_vma=False
    )
```

```python
import functools
import jax, jax.numpy as jnp
from jax import lax
from jax.sharding import PartitionSpec as P
from jax.experimental import pallas as pl
from jax.experimental.pallas import tpu as pltpu
HI = lax.Precision.HIGHEST
NT = (((1,), (1,)), ((), ()))
NN = (((1,), (0,)), ((), ()))

def dot(a, b, dims):
    return lax.dot_general(a, b, dims, precision=HI, preferred_element_type=jnp.float32)

def row_of(block, j):
    return jnp.broadcast_to(block[j:j + 1, :], (8, 128))

def recip(d):
    r = pl.reciprocal(d, approx=True)
    r = r * (2.0 - d * r)
    return r * (2.0 - d * r)

def factor_block(s_ref, w_ref, base, half_done):
    sub = lax.broadcasted_iota(jnp.int32, (8, 128), 0)
    lane = lax.broadcasted_iota(jnp.int32, (8, 128), 1)
    s = [s_ref[pl.ds(base + 8 * i, 8), :] for i in range(16)]
    w = [jnp.where(lane == sub + 8 * i, 1.0, 0.0).astype(jnp.float32) for i in range(16)]
    for p in range(16):
        col = [jnp.broadcast_to(s[p][:, 8 * p + j:8 * p + j + 1], (8, 128)) for j in range(8)]
        fac, rinv, s_rows, w_rows = {}, [], [], []
        sp, wp = s[p], w[p]
        dvec = jnp.ones((8, 128), jnp.float32)
        for j in range(8):
            d = row_of(col[j], j)
            r = recip(d)
            rinv.append(r)
            dvec = jnp.where(sub == j, d, dvec)
            m = jnp.where(sub > j, col[j] * r, 0.0)
            for k in range(j + 1, 8):
                fac[j, k] = row_of(col[k], j)
                col[k] = col[k] - m * fac[j, k]
            s_rows.append(row_of(sp, j))
            w_rows.append(row_of(wp, j))
            if j < 7:
                sp = sp - m * s_rows[j]
                wp = wp - m * w_rows[j]
        w_ref[8 * p:8 * p + 8, :] = wp * lax.rsqrt(dvec)
        for i in range(p + 1, 16):
            raw = [jnp.broadcast_to(s[i][:, 8 * p + j:8 * p + j + 1], (8, 128)) for j in range(8)]
            si, wi = s[i], w[i]
            for j in range(8):
                m = raw[j] * rinv[j]
                for k in range(j + 1, 8):
                    raw[k] = raw[k] - m * fac[j, k]
                si = si - m * s_rows[j]
                wi = wi - m * w_rows[j]
            s[i], w[i] = si, wi
        if p == 7:
            half_done()

W = (-205.0 / 72.0, 8.0 / 5.0, -1.0 / 5.0, 8.0 / 315.0, -1.0 / 560.0)

MESH = pl.DeviceIdType.MESH


def any_spec():
    return pl.BlockSpec(memory_space=pl.ANY)


STEP = 64


def shift_matrix():
    i = lax.broadcasted_iota(jnp.int32, (128, 128), 0)
    j = lax.broadcasted_iota(jnp.int32, (128, 128), 1)
    apart = jnp.abs(i - j)
    apart = jnp.minimum(apart, 128 - apart)
    out = jnp.zeros((128, 128), jnp.float32)
    for m in range(1, 5):
        out = jnp.where(apart == m, W[m], out)
    return out


def apply_level(src, pot_ref, along_z, gain, prev, put):
    w = [-0.5 * gain * c for c in W]
    shifts = along_z * (-0.5 * gain)

    def body(t, carry):
        base = t * STEP
        win = src[pl.ds(base, STEP + 8)]
        v = win[4:4 + STEP]
        acc = (gain * (pot_ref[pl.ds(base, STEP)] - 7.0) + 3.0 * w[0]) * v
        acc = acc + dot(v.reshape(STEP * 8, 128), shifts, NN).reshape(STEP, 8, 128)
        u1 = pltpu.roll(v, 1, 1) + pltpu.roll(v, 7, 1)
        r4 = pltpu.roll(v, 4, 1)
        side = [u1, pltpu.roll(v + r4, 2, 1), pltpu.roll(u1, 4, 1), r4 + r4]
        for m in range(1, 5):
            xx = win[4 + m:4 + m + STEP] + win[4 - m:4 - m + STEP]
            acc = acc + w[m] * (side[m - 1] + xx)
        if prev is not None:
            acc = acc - prev[pl.ds(base + 4, STEP)]
        put(base, acc)
        return carry

    lax.fori_loop(0, 128 // STEP, body, 0)


def fill(ref):
    ref[0:4] = ref[128:132]
    ref[132:136] = ref[4:8]


def front_kernel(orb_ref, pot_ref, m_ref, a, b, pot, c, slab,
                 send, recv, psend, precv, asend, arecv, bsend, brecv, own):
    me, my_orb = lax.axis_index("grid"), lax.axis_index("orb")
    xy, z_lo = me // 2, lax.rem(me, 2)
    z_hi, core = my_orb // 2, lax.rem(my_orb, 2)
    zc = (z_hi * 2 + z_lo) * 2 + core

    def stack(i):
        z, k = i // 2, lax.rem(i, 2)
        lo, hi = lax.rem(z, 2), z // 2
        return (xy * 2 + lo, hi * 2 + k), lo, hi, k

    bar = pltpu.get_barrier_semaphore()

    def greet(d, carry):
        pl.semaphore_signal(bar, inc=1, device_id=(lax.rem(me + d, 32), my_orb), device_id_type=MESH)
        return carry

    def greet_stack(d, carry):
        pl.semaphore_signal(bar, inc=1, device_id=stack(lax.rem(zc + d, 16))[0], device_id_type=MESH)
        return carry

    lax.fori_loop(1, 32, greet, 0)
    lax.fori_loop(1, 16, greet_stack, 0)
    pl.semaphore_wait(bar, 46)

    def orb_copy(k, d):
        to = lax.rem(me + d, 32)
        return pltpu.make_async_remote_copy(
            src_ref=orb_ref.at[2 * to + k], dst_ref=a.at[k, pl.ds(4 + 4 * me, 4)],
            send_sem=send.at[k, d], recv_sem=recv.at[k, d],
            device_id=(to, my_orb), device_id_type=MESH)

    def pot_copy(d):
        return pltpu.make_async_remote_copy(
            src_ref=pot_ref, dst_ref=pot.at[pl.ds(4 * me, 4)],
            send_sem=psend.at[d], recv_sem=precv.at[d],
            device_id=(lax.rem(me + d, 32), my_orb), device_id_type=MESH)

    def plane_copy(k, d):
        to = lax.rem(xy + d, 16)
        return pltpu.make_async_remote_copy(
            src_ref=c.at[k, pl.ds(8 * to, 8)], dst_ref=slab.at[k, xy],
            send_sem=asend.at[k, d], recv_sem=arecv.at[k, d],
            device_id=(to * 2 + z_lo, my_orb), device_id_type=MESH)

    def cell_copy(k, d):
        device, lo, hi, half = stack(lax.rem(zc + d, 16))
        return pltpu.make_async_remote_copy(
            src_ref=slab.at[k, :, 4 * lo + hi, half], dst_ref=m_ref.at[my_orb, :, z_lo, k],
            send_sem=bsend.at[k, d], recv_sem=brecv.at[k, d],
            device_id=device, device_id_type=MESH)

    def start_first(d):
        orb_copy(0, d).start()
        pot_copy(d).start()

    each(1, 32, start_first)
    each(1, 32, lambda d: orb_copy(1, d).start())
    local = [pltpu.make_async_copy(orb_ref.at[2 * me + k], a.at[k, pl.ds(4 + 4 * me, 4)], own.at[k]) for k in range(2)]
    local.append(pltpu.make_async_copy(pot_ref, pot.at[pl.ds(4 * me, 4)], own.at[2]))
    for copy in local:
        copy.start()
    for copy in local:
        copy.wait()

    def wait_pot(d):
        pot_copy(d).wait()

    each(1, 32, wait_pot)
    along_z = shift_matrix()
    for k in range(2):
        each(1, 32, lambda d: orb_copy(k, d).wait())
        ak, bk, ck = a.at[k], b.at[k], c.at[k]

        def put_b(base, value):
            bk[pl.ds(base + 4, STEP)] = value

        def put_a(base, value):
            ak[pl.ds(base + 4, STEP)] = value

        def put_c(base, value):
            ck[pl.ds(base, STEP), 0] = value[:, 0:4]
            ck[pl.ds(base, STEP), 1] = value[:, 4:8]

        fill(ak)
        apply_level(ak, pot, along_z, 0.25, None, put_b)
        fill(bk)
        apply_level(bk, pot, along_z, 0.5, ak, put_a)
        fill(ak)
        apply_level(ak, pot, along_z, 0.5, bk, put_c)
        each(1, 16, lambda d: plane_copy(k, d).start())
        mine = pltpu.make_async_copy(c.at[k, pl.ds(8 * xy, 8)], slab.at[k, xy], own.at[3 + k])
        mine.start()
        mine.wait()
    for k in range(2):
        each(1, 16, lambda d: plane_copy(k, d).wait())
        each(1, 16, lambda d: cell_copy(k, d).start())
        mine = pltpu.make_async_copy(slab.at[k, :, 4 * z_lo + z_hi, core], m_ref.at[my_orb, :, z_lo, k], own.at[5 + k])
        mine.start()
        mine.wait()
    for k in range(2):
        each(1, 16, lambda d: cell_copy(k, d).wait())


def front(orbitals, potential):
    dma, vmem, f32 = pltpu.SemaphoreType.DMA, pltpu.VMEM, jnp.float32
    return pl.pallas_call(
        front_kernel,
        out_shape=jax.ShapeDtypeStruct((8, 16, 2, 2, 4, 128), f32),
        in_specs=[any_spec()] * 2, out_specs=any_spec(),
        scratch_shapes=[vmem((2, 136, 8, 128), f32), vmem((2, 136, 8, 128), f32), vmem((128, 8, 128), f32),
                        vmem((2, 128, 2, 4, 128), f32), vmem((2, 16, 8, 2, 4, 128), f32),
                        dma((2, 32)), dma((2, 32)), dma((32,)), dma((32,)), dma((2, 16)), dma((2, 16)),
                        dma((2, 16)), dma((2, 16)), dma((7,))],
        compiler_params=pltpu.CompilerParams(collective_id=1, has_side_effects=True, vmem_limit_bytes=60 << 20),
    )(orbitals, potential)


COLUMN = (0, 4, 7, 9)
PIECES = ((0, 16), (512, 24))


def blk(i, j):
    return pl.ds(128 * (COLUMN[j] + i - j), 128)


def each(first, last, do):
    def body(d, carry):
        do(d)
        return carry
    lax.fori_loop(first, last, body, 0)


def back_kernel(cells, f_ref, out_ref, x_ref, g_ref, a_ref, y_ref, w_ref, cbuf, parts0, parts1, zparts0, zparts1,
                csend, crecv, rsend, rrecv, zsend, zrecv, gsend, grecv, esend, erecv, dsend, drecv, own):
    me, my_orb = lax.axis_index("grid"), lax.axis_index("orb")
    xy, z_lo = me // 2, lax.rem(me, 2)
    z_hi, core = my_orb // 2, lax.rem(my_orb, 2)
    z = z_hi * 2 + z_lo
    parts, zparts = (parts0, parts1), (zparts0, zparts1)
    partner = (me, z_hi * 2 + 1 - core)

    def plane(i):
        return (i * 2 + z_lo, my_orb)

    def column(i):
        return (xy * 2 + lax.rem(i, 2), (i // 2) * 2 + core)

    bar = pltpu.get_barrier_semaphore()

    def greet(device):
        pl.semaphore_signal(bar, inc=1, device_id=device, device_id_type=MESH)

    each(1, 16, lambda d: greet(plane(lax.rem(xy + d, 16))))
    each(1, 8, lambda d: greet((me, lax.rem(my_orb + d, 8))))
    each(0, 4, lambda d: greet((xy * 2 + 1 - z_lo, d * 2 + core)))

    for q in range(4):
        x_ref[:, 128 * q:128 * q + 128] = f_ref[:, q, :]

    def gram(j):
        xj = x_ref[128 * j:128 * j + 128, :]
        for i in range(j, 4):
            g_ref[blk(i, j), :] = dot(x_ref[128 * i:128 * i + 128, :], xj, NT)

    def half_rows(p, which):
        base, n = PIECES[p]
        return pl.ds(pl.multiple_of(base + 16 * n * which, 8), 16 * n)

    def own_rows(p, i):
        base, n = PIECES[p]
        return pl.ds(pl.multiple_of(base + 16 * n * core + n * i, 8), n)

    def box(p):
        return pl.ds(PIECES[p][0] // 2, 16 * PIECES[p][1])

    def core_copy(p):
        return pltpu.make_async_remote_copy(
            src_ref=g_ref.at[half_rows(p, 1 - core)], dst_ref=cbuf.at[box(p)],
            send_sem=csend.at[p], recv_sem=crecv.at[p], device_id=partner, device_id_type=MESH)

    def scatter(p, d):
        to = lax.rem(xy + d, 16)
        return pltpu.make_async_remote_copy(
            src_ref=g_ref.at[own_rows(p, to)], dst_ref=parts[p].at[xy],
            send_sem=rsend.at[p, d], recv_sem=rrecv.at[p, d], device_id=plane(to), device_id_type=MESH)

    def exchange(p, d):
        return pltpu.make_async_remote_copy(
            src_ref=zparts[p].at[z], dst_ref=zparts[p].at[z],
            send_sem=zsend.at[p, d], recv_sem=zrecv.at[p, d],
            device_id=column(lax.rem(z + d, 8)), device_id_type=MESH)

    def gather(p, d):
        return pltpu.make_async_remote_copy(
            src_ref=a_ref.at[own_rows(p, xy)], dst_ref=a_ref.at[own_rows(p, xy)],
            send_sem=gsend.at[p, d], recv_sem=grecv.at[p, d],
            device_id=plane(lax.rem(xy + d, 16)), device_id_type=MESH)

    def core_swap(p):
        return pltpu.make_async_remote_copy(
            src_ref=a_ref.at[half_rows(p, core)], dst_ref=a_ref.at[half_rows(p, core)],
            send_sem=esend.at[p], recv_sem=erecv.at[p], device_id=partner, device_id_type=MESH)

    def start_scatter(p):
        core_copy(p).wait()
        rows = half_rows(p, core)
        g_ref[rows, :] = g_ref[rows, :] + cbuf[box(p), :]
        each(1, 16, lambda d: scatter(p, d).start())
        parts[p][xy] = g_ref[own_rows(p, xy), :]

    def start_exchange(p):
        each(1, 16, lambda d: scatter(p, d).wait())
        total = parts[p][0]
        for i in range(1, 16):
            total = total + parts[p][i]
        zparts[p][z] = total
        each(1, 8, lambda d: exchange(p, d).start())

    def start_gather(p):
        each(1, 8, lambda d: exchange(p, d).wait())
        total = zparts[p][0]
        for i in range(1, 8):
            total = total + zparts[p][i]
        a_ref[own_rows(p, xy), :] = total * (1.0 / cells)
        each(1, 16, lambda d: gather(p, d).start())

    def start_swap(p):
        each(1, 16, lambda d: gather(p, d).wait())
        core_swap(p).start()

    gram(0)
    pl.semaphore_wait(bar, 26)
    core_copy(0).start()
    for j in range(1, 4):
        gram(j)
    core_copy(1).start()
    for stage in (start_scatter, start_exchange, start_gather, start_swap):
        for p in range(2):
            stage(p)
    core_swap(0).wait()

    def rows_copy(to):
        return pltpu.make_async_remote_copy(
            src_ref=y_ref.at[pl.ds(64 * to, 64)], dst_ref=out_ref.at[:, z_hi, core],
            send_sem=dsend.at[to], recv_sem=drecv.at[my_orb], device_id=(me, to), device_id_type=MESH)

    def keep(to):
        return pltpu.make_async_copy(y_ref.at[pl.ds(64 * to, 64)], out_ref.at[:, z_hi, core], own)

    def rotate_rows(b, half):
        to = 2 * b + half
        y = dot(w_ref[64 * half:64 * half + 64, :], x_ref[128 * b:128 * b + 128, :], NN)
        for q in range(4):
            y_ref[64 * to:64 * to + 64, q, :] = y[:, 128 * q:128 * q + 128]

        @pl.when(my_orb != to)
        def _():
            rows_copy(to).start()

        @pl.when(my_orb == to)
        def _():
            keep(to).start()
        return y

    for b in range(4):
        tops = []
        factor_block(a_ref, w_ref, 128 * COLUMN[b], lambda: tops.append(rotate_rows(b, 0)))
        w = w_ref[...]
        if b == 0:
            core_swap(1).wait()
        low = {}
        for i in range(b + 1, 4):
            low[i] = dot(a_ref[blk(i, b), :], w, NT)
            for j in range(b + 1, i + 1):
                a_ref[blk(i, j), :] = a_ref[blk(i, j), :] - dot(low[i], low[j], NT)
        y = jnp.concatenate([tops[0], rotate_rows(b, 1)], axis=0)
        for i in range(b + 1, 4):
            rows = slice(128 * i, 128 * i + 128)
            x_ref[rows, :] = x_ref[rows, :] - dot(low[i], y, NN)

    keep(0).wait()
    for to in range(8):
        @pl.when(my_orb != to)
        def _():
            rows_copy(to).wait_send()
    for sender in range(8):
        @pl.when(my_orb != sender)
        def _():
            pltpu.make_async_remote_copy(
                src_ref=y_ref.at[pl.ds(0, 64)], dst_ref=out_ref.at[:, sender // 2, sender % 2],
                send_sem=dsend.at[sender], recv_sem=drecv.at[sender],
                device_id=(me, sender), device_id_type=MESH).wait_recv()


def back(f, cells):
    dma, vmem, f32 = pltpu.SemaphoreType.DMA, pltpu.VMEM, jnp.float32
    return pl.pallas_call(
        functools.partial(back_kernel, cells),
        out_shape=jax.ShapeDtypeStruct((64, 4, 2, 4, 128), f32),
        in_specs=[pl.BlockSpec(memory_space=pltpu.VMEM)], out_specs=any_spec(),
        scratch_shapes=[vmem((512, 512), f32), vmem((1280, 128), f32), vmem((1280, 128), f32), vmem((512, 4, 128), f32),
                        vmem((128, 128), f32), vmem((640, 128), f32), vmem((16, 16, 128), f32), vmem((16, 24, 128), f32),
                        vmem((8, 16, 128), f32), vmem((8, 24, 128), f32),
                        dma((2,)), dma((2,)), dma((2, 16)), dma((2, 16)), dma((2, 8)), dma((2, 8)),
                        dma((2, 16)), dma((2, 16)), dma((2,)), dma((2,)), dma((8,)), dma((8,)), dma],
        compiler_params=pltpu.CompilerParams(collective_id=2, has_side_effects=True, vmem_limit_bytes=32 << 20),
    )(f)


def per_device(orbitals, potential):
    cells = front(orbitals, potential).reshape(512, 4, 128)
    return back(cells, 131072.0).reshape(64, 4, 8, 128)


def solution(mesh):
    in_specs = (P("orb", "grid", None, None), P("grid", None, None))
    out_specs = P("orb", "grid", None, None)
    return jax.shard_map(
        per_device, mesh=mesh, in_specs=in_specs, out_specs=out_specs, check_vma=False
    )
```

```python
import functools
import jax, jax.numpy as jnp
from jax import lax
from jax.sharding import PartitionSpec as P
from jax.experimental import pallas as pl
from jax.experimental.pallas import tpu as pltpu
HI = lax.Precision.HIGHEST
NT = (((1,), (1,)), ((), ()))
NN = (((1,), (0,)), ((), ()))

def dot(a, b, dims):
    return lax.dot_general(a, b, dims, precision=HI, preferred_element_type=jnp.float32)

def row_of(block, j):
    return jnp.broadcast_to(block[j:j + 1, :], (8, 128))

def recip(d):
    r = pl.reciprocal(d, approx=True)
    return r * (2.0 - d * r)

def factor_block(s_ref, w_ref, base, half_done):
    sub = lax.broadcasted_iota(jnp.int32, (8, 128), 0)
    lane = lax.broadcasted_iota(jnp.int32, (8, 128), 1)
    s = [s_ref[pl.ds(base + 8 * i, 8), :] for i in range(16)]
    w = [jnp.where(lane == sub + 8 * i, 1.0, 0.0).astype(jnp.float32) for i in range(16)]
    for p in range(16):
        col = [jnp.broadcast_to(s[p][:, 8 * p + j:8 * p + j + 1], (8, 128)) for j in range(8)]
        fac, rinv, s_rows, w_rows = {}, [], [], []
        sp, wp = s[p], w[p]
        dvec = jnp.ones((8, 128), jnp.float32)
        for j in range(8):
            d = row_of(col[j], j)
            below = jnp.where(sub > j, col[j], 0.0)
            r = recip(d)
            rinv.append(r)
            dvec = jnp.where(sub == j, d, dvec)
            m = below * r
            for k in range(j + 1, 8):
                fac[j, k] = row_of(col[k], j)
                col[k] = col[k] - m * fac[j, k]
            s_rows.append(row_of(sp, j))
            w_rows.append(row_of(wp, j))
            if j < 7:
                sp = sp - m * s_rows[j]
                wp = wp - m * w_rows[j]
        w_ref[8 * p:8 * p + 8, :] = wp * lax.rsqrt(dvec)
        for i in range(p + 1, 16):
            raw = [jnp.broadcast_to(s[i][:, 8 * p + j:8 * p + j + 1], (8, 128)) for j in range(8)]
            si, wi = s[i], w[i]
            for j in range(8):
                m = raw[j] * rinv[j]
                for k in range(j + 1, 8):
                    raw[k] = raw[k] - m * fac[j, k]
                si = si - m * s_rows[j]
                wi = wi - m * w_rows[j]
            s[i], w[i] = si, wi
        if p == 7:
            half_done()

W = (-205.0 / 72.0, 8.0 / 5.0, -1.0 / 5.0, 8.0 / 315.0, -1.0 / 560.0)

MESH = pl.DeviceIdType.MESH


def any_spec():
    return pl.BlockSpec(memory_space=pl.ANY)


STEP = 64


def shift_matrix():
    i = lax.broadcasted_iota(jnp.int32, (128, 128), 0)
    j = lax.broadcasted_iota(jnp.int32, (128, 128), 1)
    apart = jnp.abs(i - j)
    apart = jnp.minimum(apart, 128 - apart)
    out = jnp.zeros((128, 128), jnp.float32)
    for m in range(1, 5):
        out = jnp.where(apart == m, W[m], out)
    return out


def apply_level(src, pot_ref, along_z, gain, prev, put):
    w = [-0.5 * gain * c for c in W]
    shifts = along_z * (-0.5 * gain)

    def body(t, carry):
        base = t * STEP
        win = src[pl.ds(base, STEP + 8)]
        v = win[4:4 + STEP]
        acc = (gain * (pot_ref[pl.ds(base, STEP)] - 7.0) + 3.0 * w[0]) * v
        acc = acc + dot(v.reshape(STEP * 8, 128), shifts, NN).reshape(STEP, 8, 128)
        u1 = pltpu.roll(v, 1, 1) + pltpu.roll(v, 7, 1)
        r4 = pltpu.roll(v, 4, 1)
        side = [u1, pltpu.roll(v + r4, 2, 1), pltpu.roll(u1, 4, 1), r4 + r4]
        for m in range(1, 5):
            xx = win[4 + m:4 + m + STEP] + win[4 - m:4 - m + STEP]
            acc = acc + w[m] * (side[m - 1] + xx)
        if prev is not None:
            acc = acc - prev[pl.ds(base + 4, STEP)]
        put(base, acc)
        return carry

    lax.fori_loop(0, 128 // STEP, body, 0)


def fill(ref):
    ref[0:4] = ref[128:132]
    ref[132:136] = ref[4:8]


COLUMN = (0, 4, 7, 9)
PIECES = ((0, 16), (512, 24))
CELLS = 128.0 * 8.0 * 128.0


def blk(i, j):
    return pl.ds(128 * (COLUMN[j] + i - j), 128)


def each(first, last, do):
    def body(d, carry):
        do(d)
        return carry
    lax.fori_loop(first, last, body, 0)


def wait_bytes(like, sem):
    pltpu.make_async_copy(like, like, sem).wait()


def mega_kernel(orb_ref, pot_ref, out_ref, a, b, pot5, c, slab, m6, x_ref, g_ref, a_ref, y_ref, w_ref, cbuf,
                parts0, parts1, zparts0, zparts1, send, recv, psend, precv, asend, arecv, bsend, brecv, own,
                csend, crecv, rsend, rrecv, zsend, zrecv, gsend, grecv, esend, erecv, dsend, drecv):
    me, my_orb = lax.axis_index("grid"), lax.axis_index("orb")
    xy, z_lo = me // 2, lax.rem(me, 2)
    z_hi, core = my_orb // 2, lax.rem(my_orb, 2)
    z = z_hi * 2 + z_lo
    zc = z * 2 + core
    pot = pot5.reshape(128, 8, 128)
    parts, zparts = (parts0, parts1), (zparts0, zparts1)
    partner = (me, z_hi * 2 + 1 - core)

    def stack(i):
        at, k = i // 2, lax.rem(i, 2)
        lo, hi = lax.rem(at, 2), at // 2
        return (xy * 2 + lo, hi * 2 + k), lo, hi, k

    def plane(i):
        return (i * 2 + z_lo, my_orb)

    def column(i):
        return (xy * 2 + lax.rem(i, 2), (i // 2) * 2 + core)

    bar = pltpu.get_barrier_semaphore()

    def greet(device):
        pl.semaphore_signal(bar, inc=1, device_id=device, device_id_type=MESH)

    each(1, 32, lambda d: greet((lax.rem(me + d, 32), my_orb)))
    each(1, 16, lambda d: greet(stack(lax.rem(zc + d, 16))[0]))

    def remote(src, dst, send_sem, recv_sem, device):
        return pltpu.make_async_remote_copy(src_ref=src, dst_ref=dst, send_sem=send_sem, recv_sem=recv_sem,
                                            device_id=device, device_id_type=MESH)

    def pot_copy(d):
        half = pl.ds(2 * core, 2)
        remote(pot_ref.at[half], pot5.at[me, core], psend, precv, (lax.rem(me + 9 * d, 32), my_orb)).start()

    def orb_copy(k, d):
        to = lax.rem(me + 9 * d, 32)
        remote(orb_ref.at[2 * to + k], a.at[k, pl.ds(4 + 4 * me, 4)], send.at[k], recv.at[k], (to, my_orb)).start()

    pot_own = pltpu.make_async_copy(pot_ref.at[pl.ds(2 * core, 2)], pot5.at[me, core], own.at[2])
    pot_own.start()
    local = [pltpu.make_async_copy(orb_ref.at[2 * me + k], a.at[k, pl.ds(4 + 4 * me, 4)], own.at[k]) for k in range(2)]
    for copy in local:
        copy.start()
    pl.semaphore_wait(bar, 46)
    each(1, 32, pot_copy)
    each(1, 32, lambda d: orb_copy(0, d))
    each(1, 32, lambda d: orb_copy(1, d))
    pot_own.wait()
    wait_bytes(pot5.at[pl.ds(0, 31), 0], precv)
    pot_swap = remote(pot5.at[:, core], pot5.at[:, core], esend.at[2], erecv.at[2], partner)
    pot_swap.start()
    for copy in local:
        copy.wait()
    along_z = shift_matrix()

    def plane_copy(k, d):
        to = lax.rem(xy + 5 * d, 16)
        remote(c.at[k, pl.ds(8 * to, 8)], slab.at[k, xy], asend.at[k], arecv.at[k], plane(to)).start()

    def cell_copy(k, d):
        device, lo, hi, half = stack(lax.rem(zc + 7 * d, 16))
        remote(slab.at[k, :, 4 * lo + hi, half], m6.at[my_orb, :, z_lo, k], bsend.at[k], brecv.at[k], device).start()

    for k in range(2):
        wait_bytes(a.at[k, pl.ds(0, 124)], recv.at[k])
        if k == 0:
            pot_swap.wait()
        ak, bk, ck = a.at[k], b.at[k], c.at[k]

        def put_b(base, value):
            bk[pl.ds(base + 4, STEP)] = value

        def put_a(base, value):
            ak[pl.ds(base + 4, STEP)] = value

        def put_c(base, value):
            ck[pl.ds(base, STEP), 0] = value[:, 0:4]
            ck[pl.ds(base, STEP), 1] = value[:, 4:8]

        fill(ak)
        apply_level(ak, pot, along_z, 0.25, None, put_b)
        fill(bk)
        apply_level(bk, pot, along_z, 0.5, ak, put_a)
        fill(ak)
        apply_level(ak, pot, along_z, 0.5, bk, put_c)
        each(1, 16, lambda d: plane_copy(k, d))
        mine = pltpu.make_async_copy(c.at[k, pl.ds(8 * xy, 8)], slab.at[k, xy], own.at[3 + k])
        mine.start()
        mine.wait()
    for k in range(2):
        wait_bytes(slab.at[k, pl.ds(0, 15)], arecv.at[k])
        each(1, 16, lambda d: cell_copy(k, d))
        mine = pltpu.make_async_copy(slab.at[k, :, 4 * z_lo + z_hi, core], m6.at[my_orb, :, z_lo, k], own.at[5 + k])
        mine.start()
        mine.wait()
    for k in range(2):
        wait_bytes(slab.at[k, pl.ds(0, 15)], brecv.at[k])

    f_ref = m6.reshape(512, 4, 128)
    for q in range(4):
        x_ref[:, 128 * q:128 * q + 128] = f_ref[:, q, :]

    def gram(j):
        xj = x_ref[128 * j:128 * j + 128, :]
        for i in range(j, 4):
            g_ref[blk(i, j), :] = dot(x_ref[128 * i:128 * i + 128, :], xj, NT)

    def half_rows(p, which):
        base, n = PIECES[p]
        return pl.ds(pl.multiple_of(base + 16 * n * which, 8), 16 * n)

    def own_rows(p, i):
        base, n = PIECES[p]
        return pl.ds(pl.multiple_of(base + 16 * n * core + n * i, 8), n)

    def box(p):
        return pl.ds(PIECES[p][0] // 2, 16 * PIECES[p][1])

    def core_copy(p):
        return remote(g_ref.at[half_rows(p, 1 - core)], cbuf.at[box(p)], csend.at[p], crecv.at[p], partner)

    def scatter(p, d):
        to = lax.rem(xy + 5 * d, 16)
        remote(g_ref.at[own_rows(p, to)], parts[p].at[xy], rsend.at[p], rrecv.at[p], plane(to)).start()

    def exchange(p, d):
        remote(zparts[p].at[z], zparts[p].at[z], zsend.at[p], zrecv.at[p], column(lax.rem(z + 3 * d, 8))).start()

    def gather(p, d):
        rows = a_ref.at[own_rows(p, xy)]
        remote(rows, rows, gsend.at[p], grecv.at[p], plane(lax.rem(xy + 5 * d, 16))).start()

    def core_swap(p):
        rows = a_ref.at[half_rows(p, core)]
        return remote(rows, rows, esend.at[p], erecv.at[p], partner)

    def start_scatter(p):
        core_copy(p).wait()
        rows = half_rows(p, core)
        g_ref[rows, :] = g_ref[rows, :] + cbuf[box(p), :]
        each(1, 16, lambda d: scatter(p, d))
        parts[p][xy] = g_ref[own_rows(p, xy), :]

    def start_exchange(p):
        wait_bytes(parts[p].at[pl.ds(0, 15)], rrecv.at[p])
        total = parts[p][0]
        for i in range(1, 16):
            total = total + parts[p][i]
        zparts[p][z] = total
        each(1, 8, lambda d: exchange(p, d))

    def start_gather(p):
        wait_bytes(zparts[p].at[pl.ds(0, 7)], zrecv.at[p])
        total = zparts[p][0]
        for i in range(1, 8):
            total = total + zparts[p][i]
        a_ref[own_rows(p, xy), :] = total * (1.0 / CELLS)
        each(1, 16, lambda d: gather(p, d))

    def start_swap(p):
        wait_bytes(parts[p].at[pl.ds(0, 15)], grecv.at[p])
        wait_bytes(parts[p].at[pl.ds(0, 15)], gsend.at[p])
        core_swap(p).start()

    gram(0)
    core_copy(0).start()
    for j in range(1, 4):
        gram(j)
    core_copy(1).start()
    for stage in (start_scatter, start_exchange, start_gather, start_swap):
        for p in range(2):
            stage(p)
    core_swap(0).wait()

    def rows_copy(to):
        return remote(y_ref.at[pl.ds(64 * to, 64)], out_ref.at[:, z_hi, core], dsend, drecv, (me, to))

    def keep(to):
        return pltpu.make_async_copy(y_ref.at[pl.ds(64 * to, 64)], out_ref.at[:, z_hi, core], own.at[7])

    def rotate_rows(b, half):
        to = 2 * b + half
        y = dot(w_ref[64 * half:64 * half + 64, :], x_ref[128 * b:128 * b + 128, :], NN)
        for q in range(4):
            y_ref[64 * to:64 * to + 64, q, :] = y[:, 128 * q:128 * q + 128]

        @pl.when(my_orb != to)
        def _():
            rows_copy(to).start()

        @pl.when(my_orb == to)
        def _():
            keep(to).start()
        return y

    for b in range(4):
        tops = []
        factor_block(a_ref, w_ref, 128 * COLUMN[b], lambda: tops.append(rotate_rows(b, 0)))
        w = w_ref[...]
        if b == 0:
            core_swap(1).wait()
        low = {}
        for i in range(b + 1, 4):
            low[i] = dot(a_ref[blk(i, b), :], w, NT)
            for j in range(b + 1, i + 1):
                a_ref[blk(i, j), :] = a_ref[blk(i, j), :] - dot(low[i], low[j], NT)
        y = jnp.concatenate([tops[0], rotate_rows(b, 1)], axis=0)
        for i in range(b + 1, 4):
            rows = slice(128 * i, 128 * i + 128)
            x_ref[rows, :] = x_ref[rows, :] - dot(low[i], y, NN)

    wait_bytes(pot5.at[pl.ds(0, 31), 0], psend)
    for k in range(2):
        wait_bytes(a.at[k, pl.ds(0, 124)], send.at[k])
        wait_bytes(slab.at[k, pl.ds(0, 15)], asend.at[k])
        wait_bytes(slab.at[k, pl.ds(0, 15)], bsend.at[k])
    for p in range(2):
        wait_bytes(parts[p].at[pl.ds(0, 15)], rsend.at[p])
        wait_bytes(zparts[p].at[pl.ds(0, 7)], zsend.at[p])
    keep(0).wait()
    wait_bytes(y_ref.at[pl.ds(0, 448)], dsend)
    wait_bytes(y_ref.at[pl.ds(0, 448)], drecv)


def mega(orbitals, potential):
    dma, f32 = pltpu.SemaphoreType.DMA, jnp.float32

    def vmem(*shape):
        return pltpu.VMEM(shape, f32)

    return pl.pallas_call(
        mega_kernel,
        out_shape=jax.ShapeDtypeStruct((64, 4, 2, 4, 128), f32),
        in_specs=[any_spec()] * 2, out_specs=any_spec(),
        scratch_shapes=[vmem(2, 136, 8, 128), vmem(2, 136, 8, 128), vmem(32, 2, 2, 8, 128), vmem(2, 128, 2, 4, 128),
                        vmem(2, 16, 8, 2, 4, 128), vmem(8, 16, 2, 2, 4, 128),
                        vmem(512, 512), vmem(1280, 128), vmem(1280, 128), vmem(512, 4, 128), vmem(128, 128),
                        vmem(640, 128), vmem(16, 16, 128), vmem(16, 24, 128), vmem(8, 16, 128), vmem(8, 24, 128),
                        dma((2,)), dma((2,)), dma, dma, dma((2,)), dma((2,)), dma((2,)), dma((2,)), dma((8,)),
                        dma((2,)), dma((2,)), dma((2,)), dma((2,)), dma((2,)), dma((2,)),
                        dma((2,)), dma((2,)), dma((3,)), dma((3,)), dma, dma],
        compiler_params=pltpu.CompilerParams(collective_id=1, has_side_effects=True, vmem_limit_bytes=32 << 20),
    )(orbitals, potential)


def per_device(orbitals, potential):
    return mega(orbitals, potential).reshape(64, 4, 8, 128)


def solution(mesh):
    in_specs = (P("orb", "grid", None, None), P("grid", None, None))
    out_specs = P("orb", "grid", None, None)
    return jax.shard_map(
        per_device, mesh=mesh, in_specs=in_specs, out_specs=out_specs, check_vma=False
    )
```

```python
import functools
import jax, jax.numpy as jnp
from jax import lax
from jax.sharding import PartitionSpec as P
from jax.experimental import pallas as pl
from jax.experimental.pallas import tpu as pltpu
HI = lax.Precision.HIGHEST
NT = (((1,), (1,)), ((), ()))
NN = (((1,), (0,)), ((), ()))

def dot(a, b, dims):
    return lax.dot_general(a, b, dims, precision=HI, preferred_element_type=jnp.float32)

def row_of(block, j):
    return jnp.broadcast_to(block[j:j + 1, :], (8, 128))

def recip(d):
    r = pl.reciprocal(d, approx=True)
    return r * (2.0 - d * r)

def factor_block(s_ref, w_ref, base, after):
    sub = lax.broadcasted_iota(jnp.int32, (8, 128), 0)
    lane = lax.broadcasted_iota(jnp.int32, (8, 128), 1)
    s = [s_ref[pl.ds(base + 8 * i, 8), :] for i in range(16)]
    w = [jnp.where(lane == sub + 8 * i, 1.0, 0.0).astype(jnp.float32) for i in range(16)]
    for p in range(16):
        col = [jnp.broadcast_to(s[p][:, 8 * p + j:8 * p + j + 1], (8, 128)) for j in range(8)]
        fac, rinv, s_rows, w_rows = {}, [], [], []
        sp, wp = s[p], w[p]
        dvec = jnp.ones((8, 128), jnp.float32)
        first = col[0]
        for j in range(1, 8):
            first = jnp.where(sub == j, col[j], first)
        scale = pl.reciprocal(first, approx=True)

        def eliminate(j, d, r, below):
            nonlocal sp, wp, dvec
            rinv.append(r)
            dvec = jnp.where(sub == j, d, dvec)
            m = below * r
            for k in range(j + 1, 8):
                fac[j, k] = row_of(col[k], j)
                col[k] = col[k] - m * fac[j, k]
            s_rows.append(row_of(sp, j))
            w_rows.append(row_of(wp, j))
            if j < 7:
                sp = sp - m * s_rows[j]
                wp = wp - m * w_rows[j]

        for j in range(0, 8, 2):
            d0, off, d1 = row_of(col[j], j), row_of(col[j + 1], j), row_of(col[j + 1], j + 1)
            k0 = row_of(scale, j)
            d0k = d0 * k0
            both = d0k * d1 - (off * k0) * off
            r0, rb = recip(d0), recip(both)
            eliminate(j, d0, r0, jnp.where(sub > j, col[j], 0.0))
            eliminate(j + 1, both / d0k, d0k * rb, jnp.where(sub > j + 1, col[j + 1], 0.0))
        w_ref[8 * p:8 * p + 8, :] = wp * lax.rsqrt(dvec)
        for i in range(p + 1, 16):
            raw = [jnp.broadcast_to(s[i][:, 8 * p + j:8 * p + j + 1], (8, 128)) for j in range(8)]
            si, wi = s[i], w[i]
            for j in range(8):
                m = raw[j] * rinv[j]
                for k in range(j + 1, 8):
                    raw[k] = raw[k] - m * fac[j, k]
                si = si - m * s_rows[j]
                wi = wi - m * w_rows[j]
            s[i], w[i] = si, wi
        if p in after:
            after[p]()

W = (-205.0 / 72.0, 8.0 / 5.0, -1.0 / 5.0, 8.0 / 315.0, -1.0 / 560.0)

MESH = pl.DeviceIdType.MESH


def any_spec():
    return pl.BlockSpec(memory_space=pl.ANY)


STEP = 64


def shift_matrix():
    i = lax.broadcasted_iota(jnp.int32, (128, 128), 0)
    j = lax.broadcasted_iota(jnp.int32, (128, 128), 1)
    apart = jnp.abs(i - j)
    apart = jnp.minimum(apart, 128 - apart)
    out = jnp.zeros((128, 128), jnp.float32)
    for m in range(1, 5):
        out = jnp.where(apart == m, W[m], out)
    return out


def apply_level(src, pot_ref, along_z, gain, prev, put):
    w = [-0.5 * gain * c for c in W]
    shifts = along_z * (-0.5 * gain)

    def body(t, carry):
        base = t * STEP
        win = src[pl.ds(base, STEP + 8)]
        v = win[4:4 + STEP]
        acc = (gain * (pot_ref[pl.ds(base, STEP)] - 7.0) + 3.0 * w[0]) * v
        acc = acc + dot(v.reshape(STEP * 8, 128), shifts, NN).reshape(STEP, 8, 128)
        u1 = pltpu.roll(v, 1, 1) + pltpu.roll(v, 7, 1)
        r4 = pltpu.roll(v, 4, 1)
        side = [u1, pltpu.roll(v + r4, 2, 1), pltpu.roll(u1, 4, 1), r4 + r4]
        for m in range(1, 5):
            xx = win[4 + m:4 + m + STEP] + win[4 - m:4 - m + STEP]
            acc = acc + w[m] * (side[m - 1] + xx)
        if prev is not None:
            acc = acc - prev[pl.ds(base + 4, STEP)]
        put(base, acc)
        return carry

    lax.fori_loop(0, 128 // STEP, body, 0)


def fill(ref):
    ref[0:4] = ref[128:132]
    ref[132:136] = ref[4:8]


COLUMN = (0, 4, 7, 9)
PIECES = ((0, 16), (512, 24))
CELLS = 128.0 * 8.0 * 128.0


def blk(i, j):
    return pl.ds(128 * (COLUMN[j] + i - j), 128)


def each(first, last, do):
    def body(d, carry):
        do(d)
        return carry
    lax.fori_loop(first, last, body, 0)


def wait_bytes(like, sem):
    pltpu.make_async_copy(like, like, sem).wait()


def mega_kernel(orb_ref, pot_ref, out_ref, a, b, pot5, c, slab, m6, x_ref, g_ref, a_ref, y_ref, w_ref, cbuf,
                parts0, parts1, zparts0, zparts1, send, recv, psend, precv, asend, arecv, bsend, brecv, own,
                csend, crecv, rsend, rrecv, zsend, zrecv, gsend, grecv, esend, erecv, dsend, drecv):
    me, my_orb = lax.axis_index("grid"), lax.axis_index("orb")
    xy, z_lo = me // 2, lax.rem(me, 2)
    z_hi, core = my_orb // 2, lax.rem(my_orb, 2)
    z = z_hi * 2 + z_lo
    zc = z * 2 + core
    pot = pot5.reshape(128, 8, 128)
    parts, zparts = (parts0, parts1), (zparts0, zparts1)
    partner = (me, z_hi * 2 + 1 - core)

    def stack(i):
        at, k = i // 2, lax.rem(i, 2)
        lo, hi = lax.rem(at, 2), at // 2
        return (xy * 2 + lo, hi * 2 + k), lo, hi, k

    def plane(i):
        return (i * 2 + z_lo, my_orb)

    def column(i):
        return (xy * 2 + lax.rem(i, 2), (i // 2) * 2 + core)

    bar = pltpu.get_barrier_semaphore()

    def greet(device):
        pl.semaphore_signal(bar, inc=1, device_id=device, device_id_type=MESH)

    each(1, 32, lambda d: greet((lax.rem(me + d, 32), my_orb)))
    each(1, 16, lambda d: greet(stack(lax.rem(zc + d, 16))[0]))

    def remote(src, dst, send_sem, recv_sem, device):
        return pltpu.make_async_remote_copy(src_ref=src, dst_ref=dst, send_sem=send_sem, recv_sem=recv_sem,
                                            device_id=device, device_id_type=MESH)

    def pot_copy(d):
        half = pl.ds(2 * core, 2)
        remote(pot_ref.at[half], pot5.at[me, core], psend, precv, (lax.rem(me + 9 * d, 32), my_orb)).start()

    def orb_copy(k, d):
        to = lax.rem(me + 9 * d, 32)
        remote(orb_ref.at[2 * to + k], a.at[k, pl.ds(4 + 4 * me, 4)], send.at[k], recv.at[k], (to, my_orb)).start()

    pot_own = pltpu.make_async_copy(pot_ref.at[pl.ds(2 * core, 2)], pot5.at[me, core], own.at[2])
    pot_own.start()
    local = [pltpu.make_async_copy(orb_ref.at[2 * me + k], a.at[k, pl.ds(4 + 4 * me, 4)], own.at[k]) for k in range(2)]
    for copy in local:
        copy.start()
    pl.semaphore_wait(bar, 46)
    each(1, 32, pot_copy)
    each(1, 32, lambda d: orb_copy(0, d))
    each(1, 32, lambda d: orb_copy(1, d))
    pot_own.wait()
    wait_bytes(pot5.at[pl.ds(0, 31), 0], precv)
    pot_swap = remote(pot5.at[:, core], pot5.at[:, core], esend.at[2], erecv.at[2], partner)
    pot_swap.start()
    for copy in local:
        copy.wait()
    along_z = shift_matrix()

    lows = (1 - z_lo, z_lo)

    def plane_copy(k, s, d):
        to = lax.rem(xy + 5 * d, 16)
        planes = pl.ds(4 * lows[s], 4)
        remote(c.at[k, pl.ds(8 * to + 4 * lows[s], 4)], slab.at[k, xy, planes],
               asend.at[k, s], arecv.at[k, s], plane(to)).start()

    def cell_copy(k, s, d):
        to = lax.rem(my_orb + 3 * d, 8)
        remote(slab.at[k, :, 4 * lows[s] + to // 2, lax.rem(to, 2)], m6.at[my_orb, :, z_lo, k],
               bsend.at[k], brecv.at[k], (xy * 2 + lows[s], to)).start()

    for k in range(2):
        wait_bytes(a.at[k, pl.ds(0, 124)], recv.at[k])
        if k == 0:
            pot_swap.wait()
        ak, bk, ck = a.at[k], b.at[k], c.at[k]

        def put_b(base, value):
            bk[pl.ds(base + 4, STEP)] = value

        def put_a(base, value):
            ak[pl.ds(base + 4, STEP)] = value

        def put_c(base, value):
            ck[pl.ds(base, STEP), 0] = value[:, 0:4]
            ck[pl.ds(base, STEP), 1] = value[:, 4:8]

        fill(ak)
        apply_level(ak, pot, along_z, 0.25, None, put_b)
        fill(bk)
        apply_level(bk, pot, along_z, 0.5, ak, put_a)
        fill(ak)
        apply_level(ak, pot, along_z, 0.5, bk, put_c)
        for s in range(2):
            each(1, 16, lambda d: plane_copy(k, s, d))
        mine = pltpu.make_async_copy(c.at[k, pl.ds(8 * xy, 8)], slab.at[k, xy], own.at[3 + k])
        mine.start()
        mine.wait()
    for k in range(2):
        for s in range(2):
            wait_bytes(slab.at[k, pl.ds(0, 15), pl.ds(0, 4)], arecv.at[k, s])
            each(s, 8, lambda d: cell_copy(k, s, d))
        mine = pltpu.make_async_copy(slab.at[k, :, 4 * z_lo + z_hi, core], m6.at[my_orb, :, z_lo, k], own.at[5 + k])
        mine.start()
        mine.wait()
    for k in range(2):
        wait_bytes(slab.at[k, pl.ds(0, 15)], brecv.at[k])

    f_ref = m6.reshape(512, 4, 128)
    for q in range(4):
        x_ref[:, 128 * q:128 * q + 128] = f_ref[:, q, :]

    def gram(j):
        xj = x_ref[128 * j:128 * j + 128, :]
        for i in range(j, 4):
            g_ref[blk(i, j), :] = dot(x_ref[128 * i:128 * i + 128, :], xj, NT)

    def half_rows(p, which):
        base, n = PIECES[p]
        return pl.ds(pl.multiple_of(base + 16 * n * which, 8), 16 * n)

    def own_rows(p, i):
        base, n = PIECES[p]
        return pl.ds(pl.multiple_of(base + 16 * n * core + n * i, 8), n)

    def box(p):
        return pl.ds(PIECES[p][0] // 2, 16 * PIECES[p][1])

    def core_copy(p):
        return remote(g_ref.at[half_rows(p, 1 - core)], cbuf.at[box(p)], csend.at[p], crecv.at[p], partner)

    def scatter(p, d):
        to = lax.rem(xy + 5 * d, 16)
        remote(g_ref.at[own_rows(p, to)], parts[p].at[xy], rsend.at[p], rrecv.at[p], plane(to)).start()

    def exchange(p, d):
        remote(zparts[p].at[z], zparts[p].at[z], zsend.at[p], zrecv.at[p], column(lax.rem(z + 3 * d, 8))).start()

    def gather(p, d):
        rows = a_ref.at[own_rows(p, xy)]
        remote(rows, rows, gsend.at[p], grecv.at[p], plane(lax.rem(xy + 5 * d, 16))).start()

    def core_swap(p):
        rows = a_ref.at[half_rows(p, core)]
        return remote(rows, rows, esend.at[p], erecv.at[p], partner)

    def start_scatter(p):
        core_copy(p).wait()
        rows = half_rows(p, core)
        g_ref[rows, :] = g_ref[rows, :] + cbuf[box(p), :]
        each(1, 16, lambda d: scatter(p, d))
        parts[p][xy] = g_ref[own_rows(p, xy), :]

    def start_exchange(p):
        wait_bytes(parts[p].at[pl.ds(0, 15)], rrecv.at[p])
        total = parts[p][0]
        for i in range(1, 16):
            total = total + parts[p][i]
        zparts[p][z] = total
        each(1, 8, lambda d: exchange(p, d))

    def start_gather(p):
        wait_bytes(zparts[p].at[pl.ds(0, 7)], zrecv.at[p])
        total = zparts[p][0]
        for i in range(1, 8):
            total = total + zparts[p][i]
        a_ref[own_rows(p, xy), :] = total * (1.0 / CELLS)
        each(1, 16, lambda d: gather(p, d))

    def start_swap(p):
        wait_bytes(parts[p].at[pl.ds(0, 15)], grecv.at[p])
        wait_bytes(parts[p].at[pl.ds(0, 15)], gsend.at[p])
        core_swap(p).start()

    gram(0)
    core_copy(0).start()
    for j in range(1, 4):
        gram(j)
    core_copy(1).start()
    for stage in (start_scatter, start_exchange, start_gather, start_swap):
        for p in range(2):
            stage(p)
    core_swap(0).wait()

    def rows_copy(to):
        return remote(y_ref.at[pl.ds(64 * to, 64)], out_ref.at[:, z_hi, core], dsend, drecv, (me, to))

    def keep(to):
        return pltpu.make_async_copy(y_ref.at[pl.ds(64 * to, 64)], out_ref.at[:, z_hi, core], own.at[7])

    def rotate_rows(b, half):
        to = 2 * b + half
        y = dot(w_ref[64 * half:64 * half + 64, :], x_ref[128 * b:128 * b + 128, :], NN)
        for q in range(4):
            y_ref[64 * to:64 * to + 64, q, :] = y[:, 128 * q:128 * q + 128]

        @pl.when(my_orb != to)
        def _():
            rows_copy(to).start()

        @pl.when(my_orb == to)
        def _():
            keep(to).start()
        return y

    soon, later = [], []
    for b in range(4):
        tops = []

        def run(work):
            while work:
                work.pop(0)()

        factor_block(a_ref, w_ref, 128 * COLUMN[b], {
            0: lambda: run(soon), 7: lambda: tops.append(rotate_rows(b, 0)), 8: lambda: run(later)})
        w = w_ref[...]
        if b == 0:
            core_swap(1).wait()
        low = {}

        def lower(i, b=b, w=w, low=low):
            low[i] = dot(a_ref[blk(i, b), :], w, NT)

        def update(i, j, low=low):
            a_ref[blk(i, j), :] = a_ref[blk(i, j), :] - dot(low[i], low[j], NT)

        if b < 3:
            lower(b + 1)
            update(b + 1, b + 1)
        y = jnp.concatenate([tops[0], rotate_rows(b, 1)], axis=0)

        def solve(i, y=y, low=low):
            rows = slice(128 * i, 128 * i + 128)
            x_ref[rows, :] = x_ref[rows, :] - dot(low[i], y, NN)

        for i in range(b + 1, 4):
            if i > b + 1:
                later.append(functools.partial(lower, i))
                for j in range(b + 1, i + 1):
                    later.append(functools.partial(update, i, j))
            (later if i > b + 1 else soon).append(functools.partial(solve, i))

    wait_bytes(pot5.at[pl.ds(0, 31), 0], psend)
    for k in range(2):
        wait_bytes(a.at[k, pl.ds(0, 124)], send.at[k])
        for s in range(2):
            wait_bytes(slab.at[k, pl.ds(0, 15), pl.ds(0, 4)], asend.at[k, s])
        wait_bytes(slab.at[k, pl.ds(0, 15)], bsend.at[k])
    for p in range(2):
        wait_bytes(parts[p].at[pl.ds(0, 15)], rsend.at[p])
        wait_bytes(zparts[p].at[pl.ds(0, 7)], zsend.at[p])
    keep(0).wait()
    wait_bytes(y_ref.at[pl.ds(0, 448)], dsend)
    wait_bytes(y_ref.at[pl.ds(0, 448)], drecv)


def mega(orbitals, potential):
    dma, f32 = pltpu.SemaphoreType.DMA, jnp.float32

    def vmem(*shape):
        return pltpu.VMEM(shape, f32)

    return pl.pallas_call(
        mega_kernel,
        out_shape=jax.ShapeDtypeStruct((64, 4, 2, 4, 128), f32),
        in_specs=[any_spec()] * 2, out_specs=any_spec(),
        scratch_shapes=[vmem(2, 136, 8, 128), vmem(2, 136, 8, 128), vmem(32, 2, 2, 8, 128), vmem(2, 128, 2, 4, 128),
                        vmem(2, 16, 8, 2, 4, 128), vmem(8, 16, 2, 2, 4, 128),
                        vmem(512, 512), vmem(1280, 128), vmem(1280, 128), vmem(512, 4, 128), vmem(128, 128),
                        vmem(640, 128), vmem(16, 16, 128), vmem(16, 24, 128), vmem(8, 16, 128), vmem(8, 24, 128),
                        dma((2,)), dma((2,)), dma, dma, dma((2, 2)), dma((2, 2)), dma((2,)), dma((2,)), dma((8,)),
                        dma((2,)), dma((2,)), dma((2,)), dma((2,)), dma((2,)), dma((2,)),
                        dma((2,)), dma((2,)), dma((3,)), dma((3,)), dma, dma],
        compiler_params=pltpu.CompilerParams(collective_id=1, has_side_effects=True, vmem_limit_bytes=32 << 20),
    )(orbitals, potential)


def per_device(orbitals, potential):
    return mega(orbitals, potential).reshape(64, 4, 8, 128)


def solution(mesh):
    in_specs = (P("orb", "grid", None, None), P("grid", None, None))
    out_specs = P("orb", "grid", None, None)
    return jax.shard_map(
        per_device, mesh=mesh, in_specs=in_specs, out_specs=out_specs, check_vma=False
    )
```

```python
import functools
import jax, jax.numpy as jnp
from jax import lax
from jax.sharding import PartitionSpec as P
from jax.experimental import pallas as pl
from jax.experimental.pallas import tpu as pltpu
HI = lax.Precision.HIGHEST
NT = (((1,), (1,)), ((), ()))
NN = (((1,), (0,)), ((), ()))

def dot(a, b, dims):
    return lax.dot_general(a, b, dims, precision=HI, preferred_element_type=jnp.float32)

def row_of(block, j):
    return jnp.broadcast_to(block[j:j + 1, :], (8, 128))

def recip(d):
    r = pl.reciprocal(d, approx=True)
    return r * (2.0 - d * r)

def factor_block(s_ref, w_ref, base, after):
    sub = lax.broadcasted_iota(jnp.int32, (8, 128), 0)
    lane = lax.broadcasted_iota(jnp.int32, (8, 128), 1)
    s = [s_ref[pl.ds(base + 8 * i, 8), :] for i in range(16)]
    w = [jnp.where(lane == sub + 8 * i, 1.0, 0.0).astype(jnp.float32) for i in range(16)]
    for p in range(16):
        col = [jnp.broadcast_to(s[p][:, 8 * p + j:8 * p + j + 1], (8, 128)) for j in range(8)]
        fac, rinv, s_rows, w_rows = {}, [], [], []
        sp, wp = s[p], w[p]
        dvec = jnp.ones((8, 128), jnp.float32)
        first = col[0]
        for j in range(1, 8):
            first = jnp.where(sub == j, col[j], first)
        scale = pl.reciprocal(first, approx=True)

        def eliminate(j, d, r, below):
            nonlocal sp, wp, dvec
            rinv.append(r)
            dvec = jnp.where(sub == j, d, dvec)
            m = below * r
            for k in range(j + 1, 8):
                fac[j, k] = row_of(col[k], j)
                col[k] = col[k] - m * fac[j, k]
            s_rows.append(row_of(sp, j))
            w_rows.append(row_of(wp, j))
            if j < 7:
                sp = sp - m * s_rows[j]
                wp = wp - m * w_rows[j]

        for j in range(0, 8, 2):
            d0, off, d1 = row_of(col[j], j), row_of(col[j + 1], j), row_of(col[j + 1], j + 1)
            k0 = row_of(scale, j)
            d0k = d0 * k0
            both = d0k * d1 - (off * k0) * off
            r0, rb = recip(d0), recip(both)
            eliminate(j, d0, r0, jnp.where(sub > j, col[j], 0.0))
            eliminate(j + 1, both / d0k, d0k * rb, jnp.where(sub > j + 1, col[j + 1], 0.0))
        w_ref[8 * p:8 * p + 8, :] = wp * lax.rsqrt(dvec)
        for i in range(p + 1, 16):
            raw = [jnp.broadcast_to(s[i][:, 8 * p + j:8 * p + j + 1], (8, 128)) for j in range(8)]
            si, wi = s[i], w[i]
            for j in range(8):
                m = raw[j] * rinv[j]
                for k in range(j + 1, 8):
                    raw[k] = raw[k] - m * fac[j, k]
                si = si - m * s_rows[j]
                wi = wi - m * w_rows[j]
            s[i], w[i] = si, wi
        if p in after:
            after[p]()

W = (-205.0 / 72.0, 8.0 / 5.0, -1.0 / 5.0, 8.0 / 315.0, -1.0 / 560.0)

MESH = pl.DeviceIdType.MESH


def any_spec():
    return pl.BlockSpec(memory_space=pl.ANY)


STEP = 64


def shift_matrix():
    i = lax.broadcasted_iota(jnp.int32, (128, 128), 0)
    j = lax.broadcasted_iota(jnp.int32, (128, 128), 1)
    apart = jnp.abs(i - j)
    apart = jnp.minimum(apart, 128 - apart)
    out = jnp.zeros((128, 128), jnp.float32)
    for m in range(1, 5):
        out = jnp.where(apart == m, W[m], out)
    return out


def apply_level(src, pot_ref, along_z, gain, prev, put):
    w = [-0.5 * gain * c for c in W]
    shifts = along_z * (-0.5 * gain)

    def body(t, carry):
        base = t * STEP
        win = src[pl.ds(base, STEP + 8)]
        v = win[4:4 + STEP]
        acc = (gain * (pot_ref[pl.ds(base, STEP)] - 7.0) + 3.0 * w[0]) * v
        acc = acc + dot(v.reshape(STEP * 8, 128), shifts, NN).reshape(STEP, 8, 128)
        u1 = pltpu.roll(v, 1, 1) + pltpu.roll(v, 7, 1)
        r4 = pltpu.roll(v, 4, 1)
        side = [u1, pltpu.roll(v + r4, 2, 1), pltpu.roll(u1, 4, 1), r4 + r4]
        for m in range(1, 5):
            xx = win[4 + m:4 + m + STEP] + win[4 - m:4 - m + STEP]
            acc = acc + w[m] * (side[m - 1] + xx)
        if prev is not None:
            acc = acc - prev[pl.ds(base + 4, STEP)]
        put(base, acc)
        return carry

    lax.fori_loop(0, 128 // STEP, body, 0)


def fill(ref):
    ref[0:4] = ref[128:132]
    ref[132:136] = ref[4:8]


COLUMN = (0, 4, 7, 9)
PIECES = ((0, 16), (512, 24))
CELLS = 128.0 * 8.0 * 128.0


def blk(i, j):
    return pl.ds(128 * (COLUMN[j] + i - j), 128)


def each(first, last, do):
    def body(d, carry):
        do(d)
        return carry
    lax.fori_loop(first, last, body, 0)


def wait_bytes(like, sem):
    pltpu.make_async_copy(like, like, sem).wait()


def mega_kernel(orb_ref, pot_ref, out_ref, a, b, pot5, c, slab, m6, x_ref, g_ref, a_ref, y_ref, w_ref, cbuf,
                parts0, parts1, zparts0, zparts1, send, recv, psend, precv, asend, arecv, bsend, brecv, own,
                csend, crecv, rsend, rrecv, zsend, zrecv, gsend, grecv, esend, erecv, dsend, drecv):
    me, my_orb = lax.axis_index("grid"), lax.axis_index("orb")
    xy, z_lo = me // 2, lax.rem(me, 2)
    z_hi, core = my_orb // 2, lax.rem(my_orb, 2)
    z = z_hi * 2 + z_lo
    zc = z * 2 + core
    pot = pot5.reshape(128, 8, 128)
    parts, zparts = (parts0, parts1), (zparts0, zparts1)
    partner = (me, z_hi * 2 + 1 - core)

    def stack(i):
        at, k = i // 2, lax.rem(i, 2)
        lo, hi = lax.rem(at, 2), at // 2
        return (xy * 2 + lo, hi * 2 + k), lo, hi, k

    def plane(i):
        return (i * 2 + z_lo, my_orb)

    def column(i):
        return (xy * 2 + lax.rem(i, 2), (i // 2) * 2 + core)

    bar = pltpu.get_barrier_semaphore()

    def greet(device):
        pl.semaphore_signal(bar, inc=1, device_id=device, device_id_type=MESH)

    each(1, 32, lambda d: greet((lax.rem(me + d, 32), my_orb)))
    each(1, 16, lambda d: greet(stack(lax.rem(zc + d, 16))[0]))

    def remote(src, dst, send_sem, recv_sem, device):
        return pltpu.make_async_remote_copy(src_ref=src, dst_ref=dst, send_sem=send_sem, recv_sem=recv_sem,
                                            device_id=device, device_id_type=MESH)

    def pot_copy(d):
        half = pl.ds(2 * core, 2)
        remote(pot_ref.at[half], pot5.at[me, core], psend, precv, (lax.rem(me + 9 * d, 32), my_orb)).start()

    def orb_copy(k, d):
        to = lax.rem(me + 9 * d, 32)
        remote(orb_ref.at[2 * to + k], a.at[k, pl.ds(4 + 4 * me, 4)], send.at[k], recv.at[k], (to, my_orb)).start()

    pot_own = pltpu.make_async_copy(pot_ref.at[pl.ds(2 * core, 2)], pot5.at[me, core], own.at[2])
    pot_own.start()
    local = [pltpu.make_async_copy(orb_ref.at[2 * me + k], a.at[k, pl.ds(4 + 4 * me, 4)], own.at[k]) for k in range(2)]
    for copy in local:
        copy.start()
    pl.semaphore_wait(bar, 46)
    each(1, 32, pot_copy)
    each(1, 32, lambda d: orb_copy(0, d))
    each(1, 32, lambda d: orb_copy(1, d))
    pot_own.wait()
    wait_bytes(pot5.at[pl.ds(0, 31), 0], precv)
    pot_swap = remote(pot5.at[:, core], pot5.at[:, core], esend.at[2], erecv.at[2], partner)
    pot_swap.start()
    for copy in local:
        copy.wait()
    along_z = shift_matrix()

    lows = (1 - z_lo, z_lo)

    def plane_copy(k, s, d):
        to = lax.rem(xy + 5 * d, 16)
        planes = pl.ds(4 * lows[s], 4)
        remote(c.at[k, pl.ds(8 * to + 4 * lows[s], 4)], slab.at[k, xy, planes],
               asend.at[k, s], arecv.at[k, s], plane(to)).start()

    def cell_copy(k, s, d):
        to = lax.rem(my_orb + 3 * d, 8)
        remote(slab.at[k, :, 4 * lows[s] + to // 2, lax.rem(to, 2)], m6.at[my_orb, :, z_lo, k],
               bsend.at[k], brecv.at[k], (xy * 2 + lows[s], to)).start()

    for k in range(2):
        wait_bytes(a.at[k, pl.ds(0, 124)], recv.at[k])
        if k == 0:
            pot_swap.wait()
        ak, bk, ck = a.at[k], b.at[k], c.at[k]

        def put_b(base, value):
            bk[pl.ds(base + 4, STEP)] = value

        def put_a(base, value):
            ak[pl.ds(base + 4, STEP)] = value

        def put_c(base, value):
            ck[pl.ds(base, STEP), 0] = value[:, 0:4]
            ck[pl.ds(base, STEP), 1] = value[:, 4:8]

        fill(ak)
        apply_level(ak, pot, along_z, 0.25, None, put_b)
        fill(bk)
        apply_level(bk, pot, along_z, 0.5, ak, put_a)
        fill(ak)
        apply_level(ak, pot, along_z, 0.5, bk, put_c)
        for s in range(2):
            each(1, 16, lambda d: plane_copy(k, s, d))
        mine = pltpu.make_async_copy(c.at[k, pl.ds(8 * xy, 8)], slab.at[k, xy], own.at[3 + k])
        mine.start()
        mine.wait()
    for k in range(2):
        for s in range(2):
            wait_bytes(slab.at[k, pl.ds(0, 15), pl.ds(0, 4)], arecv.at[k, s])
            each(s, 8, lambda d: cell_copy(k, s, d))
        mine = pltpu.make_async_copy(slab.at[k, :, 4 * z_lo + z_hi, core], m6.at[my_orb, :, z_lo, k], own.at[5 + k])
        mine.start()
        mine.wait()
    for k in range(2):
        wait_bytes(slab.at[k, pl.ds(0, 15)], brecv.at[k])

    f_ref = m6.reshape(512, 4, 128)
    for q in range(4):
        x_ref[:, 128 * q:128 * q + 128] = f_ref[:, q, :]

    def gram(j):
        xj = x_ref[128 * j:128 * j + 128, :]
        for i in range(j, 4):
            g_ref[blk(i, j), :] = dot(x_ref[128 * i:128 * i + 128, :], xj, NT)

    def half_rows(p, which):
        base, n = PIECES[p]
        return pl.ds(pl.multiple_of(base + 16 * n * which, 8), 16 * n)

    def own_rows(p, i):
        base, n = PIECES[p]
        return pl.ds(pl.multiple_of(base + 16 * n * core + n * i, 8), n)

    def box(p):
        return pl.ds(PIECES[p][0] // 2, 16 * PIECES[p][1])

    def core_copy(p):
        return remote(g_ref.at[half_rows(p, 1 - core)], cbuf.at[box(p)], csend.at[p], crecv.at[p], partner)

    def scatter(p, d):
        to = lax.rem(xy + 5 * d, 16)
        remote(g_ref.at[own_rows(p, to)], parts[p].at[xy], rsend.at[p], rrecv.at[p], plane(to)).start()

    def exchange(p, d):
        remote(zparts[p].at[z], zparts[p].at[z], zsend.at[p], zrecv.at[p], column(lax.rem(z + 3 * d, 8))).start()

    def gather(p, d):
        rows = a_ref.at[own_rows(p, xy)]
        remote(rows, rows, gsend.at[p], grecv.at[p], plane(lax.rem(xy + 5 * d, 16))).start()

    def core_swap(p):
        rows = a_ref.at[half_rows(p, core)]
        return remote(rows, rows, esend.at[p], erecv.at[p], partner)

    def start_scatter(p):
        core_copy(p).wait()
        rows = half_rows(p, core)
        g_ref[rows, :] = g_ref[rows, :] + cbuf[box(p), :]
        each(1, 16, lambda d: scatter(p, d))
        parts[p][xy] = g_ref[own_rows(p, xy), :]

    def start_exchange(p):
        wait_bytes(parts[p].at[pl.ds(0, 15)], rrecv.at[p])
        total = parts[p][0]
        for i in range(1, 16):
            total = total + parts[p][i]
        zparts[p][z] = total
        each(1, 8, lambda d: exchange(p, d))

    def start_gather(p):
        wait_bytes(zparts[p].at[pl.ds(0, 7)], zrecv.at[p])
        total = zparts[p][0]
        for i in range(1, 8):
            total = total + zparts[p][i]
        a_ref[own_rows(p, xy), :] = total * (1.0 / CELLS)
        each(1, 16, lambda d: gather(p, d))

    def start_swap(p):
        wait_bytes(parts[p].at[pl.ds(0, 15)], grecv.at[p])
        wait_bytes(parts[p].at[pl.ds(0, 15)], gsend.at[p])
        core_swap(p).start()

    gram(0)
    core_copy(0).start()
    for j in range(1, 4):
        gram(j)
    core_copy(1).start()
    for stage in (start_scatter, start_exchange, start_gather, start_swap):
        for p in range(2):
            stage(p)
    core_swap(0).wait()

    def ends(to, first, count):
        rows = y_ref.at[pl.ds(64 * to + first, count)]
        return rows, out_ref.at[pl.ds(first, count), z_hi, core]

    def rotate_rows(b, start, count):
        to, first = 2 * b + start // 64, start % 64
        y = dot(w_ref[start:start + count, :], x_ref[128 * b:128 * b + 128, :], NN)
        for q in range(4):
            y_ref[128 * b + start:128 * b + start + count, q, :] = y[:, 128 * q:128 * q + 128]
        rows, place = ends(to, first, count)

        @pl.when(my_orb != to)
        def _():
            remote(rows, place, dsend, drecv, (me, to)).start()

        @pl.when(my_orb == to)
        def _():
            pltpu.make_async_copy(rows, place, own.at[7]).start()
        return y

    soon, later = [], []
    for b in range(4):
        tops = []

        def run(work):
            while work:
                work.pop(0)()

        count = 32 if b == 3 else 64
        after = {0: lambda: run(soon), 8: lambda: run(later)}
        for start in range(0, 128 - count, count):
            after[(start + count) // 8 - 1] = lambda start=start: tops.append(rotate_rows(b, start, count))
        factor_block(a_ref, w_ref, 128 * COLUMN[b], after)
        w = w_ref[...]
        if b == 0:
            core_swap(1).wait()
        low = {}

        def lower(i, b=b, w=w, low=low):
            low[i] = dot(a_ref[blk(i, b), :], w, NT)

        def update(i, j, low=low):
            a_ref[blk(i, j), :] = a_ref[blk(i, j), :] - dot(low[i], low[j], NT)

        if b < 3:
            lower(b + 1)
            update(b + 1, b + 1)
        tops.append(rotate_rows(b, 128 - count, count))
        y = jnp.concatenate(tops, axis=0) if b < 3 else None

        def solve(i, y=y, low=low):
            rows = slice(128 * i, 128 * i + 128)
            x_ref[rows, :] = x_ref[rows, :] - dot(low[i], y, NN)

        for i in range(b + 1, 4):
            if i > b + 1:
                later.append(functools.partial(lower, i))
                for j in range(b + 1, i + 1):
                    later.append(functools.partial(update, i, j))
            (later if i > b + 1 else soon).append(functools.partial(solve, i))

    wait_bytes(pot5.at[pl.ds(0, 31), 0], psend)
    for k in range(2):
        wait_bytes(a.at[k, pl.ds(0, 124)], send.at[k])
        for s in range(2):
            wait_bytes(slab.at[k, pl.ds(0, 15), pl.ds(0, 4)], asend.at[k, s])
        wait_bytes(slab.at[k, pl.ds(0, 15)], bsend.at[k])
    for p in range(2):
        wait_bytes(parts[p].at[pl.ds(0, 15)], rsend.at[p])
        wait_bytes(zparts[p].at[pl.ds(0, 7)], zsend.at[p])
    wait_bytes(y_ref.at[pl.ds(0, 64)], own.at[7])
    wait_bytes(y_ref.at[pl.ds(0, 448)], dsend)
    wait_bytes(y_ref.at[pl.ds(0, 448)], drecv)


def mega(orbitals, potential):
    dma, f32 = pltpu.SemaphoreType.DMA, jnp.float32

    def vmem(*shape):
        return pltpu.VMEM(shape, f32)

    return pl.pallas_call(
        mega_kernel,
        out_shape=jax.ShapeDtypeStruct((64, 4, 2, 4, 128), f32),
        in_specs=[any_spec()] * 2, out_specs=any_spec(),
        scratch_shapes=[vmem(2, 136, 8, 128), vmem(2, 136, 8, 128), vmem(32, 2, 2, 8, 128), vmem(2, 128, 2, 4, 128),
                        vmem(2, 16, 8, 2, 4, 128), vmem(8, 16, 2, 2, 4, 128),
                        vmem(512, 512), vmem(1280, 128), vmem(1280, 128), vmem(512, 4, 128), vmem(128, 128),
                        vmem(640, 128), vmem(16, 16, 128), vmem(16, 24, 128), vmem(8, 16, 128), vmem(8, 24, 128),
                        dma((2,)), dma((2,)), dma, dma, dma((2, 2)), dma((2, 2)), dma((2,)), dma((2,)), dma((8,)),
                        dma((2,)), dma((2,)), dma((2,)), dma((2,)), dma((2,)), dma((2,)),
                        dma((2,)), dma((2,)), dma((3,)), dma((3,)), dma, dma],
        compiler_params=pltpu.CompilerParams(collective_id=1, has_side_effects=True, vmem_limit_bytes=52 << 20),
    )(orbitals, potential)


def per_device(orbitals, potential):
    return mega(orbitals, potential).reshape(64, 4, 8, 128)


def solution(mesh):
    in_specs = (P("orb", "grid", None, None), P("grid", None, None))
    out_specs = P("orb", "grid", None, None)
    return jax.shard_map(
        per_device, mesh=mesh, in_specs=in_specs, out_specs=out_specs, check_vma=False
    )
```

```python
import functools
import jax, jax.numpy as jnp
from jax import lax
from jax.sharding import PartitionSpec as P
from jax.experimental import pallas as pl
from jax.experimental.pallas import tpu as pltpu
HI = lax.Precision.HIGHEST
NT = (((1,), (1,)), ((), ()))
NN = (((1,), (0,)), ((), ()))

def dot(a, b, dims):
    return lax.dot_general(a, b, dims, precision=HI, preferred_element_type=jnp.float32)

def row_of(block, j):
    return jnp.broadcast_to(block[j:j + 1, :], (8, 128))

def recip(d):
    r = pl.reciprocal(d, approx=True)
    return r * (2.0 - d * r)

def factor_block(s_ref, w_ref, base, after):
    sub = lax.broadcasted_iota(jnp.int32, (8, 128), 0)
    lane = lax.broadcasted_iota(jnp.int32, (8, 128), 1)
    s = [s_ref[pl.ds(base + 8 * i, 8), :] for i in range(16)]
    w = [jnp.where(lane == sub + 8 * i, 1.0, 0.0).astype(jnp.float32) for i in range(16)]
    for p in range(16):
        col = [jnp.broadcast_to(s[p][:, 8 * p + j:8 * p + j + 1], (8, 128)) for j in range(8)]
        fac, rinv, s_rows, w_rows = {}, [], [], []
        sp, wp = s[p], w[p]
        dvec = jnp.ones((8, 128), jnp.float32)
        first = col[0]
        for j in range(1, 8):
            first = jnp.where(sub == j, col[j], first)
        scale = pl.reciprocal(first, approx=True)

        def eliminate(j, d, r, below):
            nonlocal sp, wp, dvec
            rinv.append(r)
            dvec = jnp.where(sub == j, d, dvec)
            m = below * r
            for k in range(j + 1, 8):
                fac[j, k] = row_of(col[k], j)
                col[k] = col[k] - m * fac[j, k]
            s_rows.append(row_of(sp, j))
            w_rows.append(row_of(wp, j))
            if j < 7:
                sp = sp - m * s_rows[j]
                wp = wp - m * w_rows[j]

        for j in range(0, 8, 2):
            d0, off, d1 = row_of(col[j], j), row_of(col[j + 1], j), row_of(col[j + 1], j + 1)
            k0 = row_of(scale, j)
            d0k = d0 * k0
            both = d0k * d1 - (off * k0) * off
            r0, rb = recip(d0), recip(both)
            eliminate(j, d0, r0, jnp.where(sub > j, col[j], 0.0))
            eliminate(j + 1, both / d0k, d0k * rb, jnp.where(sub > j + 1, col[j + 1], 0.0))
        w_ref[8 * p:8 * p + 8, :] = wp * lax.rsqrt(dvec)
        for i in range(p + 1, 16):
            raw = [jnp.broadcast_to(s[i][:, 8 * p + j:8 * p + j + 1], (8, 128)) for j in range(8)]
            si, wi = s[i], w[i]
            for j in range(8):
                m = raw[j] * rinv[j]
                for k in range(j + 1, 8):
                    raw[k] = raw[k] - m * fac[j, k]
                si = si - m * s_rows[j]
                wi = wi - m * w_rows[j]
            s[i], w[i] = si, wi
        if p in after:
            after[p]()

W = (-205.0 / 72.0, 8.0 / 5.0, -1.0 / 5.0, 8.0 / 315.0, -1.0 / 560.0)

MESH = pl.DeviceIdType.MESH


def any_spec():
    return pl.BlockSpec(memory_space=pl.ANY)


STEP = 64


def shift_matrix():
    i = lax.broadcasted_iota(jnp.int32, (128, 128), 0)
    j = lax.broadcasted_iota(jnp.int32, (128, 128), 1)
    apart = jnp.abs(i - j)
    apart = jnp.minimum(apart, 128 - apart)
    out = jnp.zeros((128, 128), jnp.float32)
    for m in range(1, 5):
        out = jnp.where(apart == m, W[m], out)
    return out


def apply_level(src, pot_ref, along_z, gain, prev, put):
    w = [-0.5 * gain * c for c in W]
    shifts = along_z * (-0.5 * gain)

    def body(t, carry):
        base = t * STEP
        win = src[pl.ds(base, STEP + 8)]
        v = win[4:4 + STEP]
        acc = (gain * (pot_ref[pl.ds(base, STEP)] - 7.0) + 3.0 * w[0]) * v
        acc = acc + dot(v.reshape(STEP * 8, 128), shifts, NN).reshape(STEP, 8, 128)
        u1 = pltpu.roll(v, 1, 1) + pltpu.roll(v, 7, 1)
        r4 = pltpu.roll(v, 4, 1)
        side = [u1, pltpu.roll(v + r4, 2, 1), pltpu.roll(u1, 4, 1), r4 + r4]
        for m in range(1, 5):
            xx = win[4 + m:4 + m + STEP] + win[4 - m:4 - m + STEP]
            acc = acc + w[m] * (side[m - 1] + xx)
        if prev is not None:
            acc = acc - prev[pl.ds(base + 4, STEP)]
        put(base, acc)
        return carry

    lax.fori_loop(0, 128 // STEP, body, 0)


def fill(ref):
    ref[0:4] = ref[128:132]
    ref[132:136] = ref[4:8]


COLUMN = (0, 4, 7, 9)
PIECES = ((0, 16), (512, 24))
CELLS = 128.0 * 8.0 * 128.0


def blk(i, j):
    return pl.ds(128 * (COLUMN[j] + i - j), 128)


def each(first, last, do):
    def body(d, carry):
        do(d)
        return carry
    lax.fori_loop(first, last, body, 0, unroll=True)


def wait_bytes(like, sem):
    pltpu.make_async_copy(like, like, sem).wait()


def mega_kernel(orb_ref, pot_ref, out_ref, a, b, pot5, c, slab, m6, x_ref, g_ref, a_ref, y_ref, w_ref, cbuf,
                parts0, parts1, zparts0, zparts1, send, recv, psend, precv, asend, arecv, bsend, brecv, own,
                csend, crecv, rsend, rrecv, zsend, zrecv, gsend, grecv, esend, erecv, dsend, drecv):
    me, my_orb = lax.axis_index("grid"), lax.axis_index("orb")
    xy, z_lo = me // 2, lax.rem(me, 2)
    z_hi, core = my_orb // 2, lax.rem(my_orb, 2)
    z = z_hi * 2 + z_lo
    zc = z * 2 + core
    pot = pot5.reshape(128, 8, 128)
    parts, zparts = (parts0, parts1), (zparts0, zparts1)
    partner = (me, z_hi * 2 + 1 - core)

    def stack(i):
        at, k = i // 2, lax.rem(i, 2)
        lo, hi = lax.rem(at, 2), at // 2
        return (xy * 2 + lo, hi * 2 + k), lo, hi, k

    def plane(i):
        return (i * 2 + z_lo, my_orb)

    def column(i):
        return (xy * 2 + lax.rem(i, 2), (i // 2) * 2 + core)

    bar = pltpu.get_barrier_semaphore()

    def greet(device):
        pl.semaphore_signal(bar, inc=1, device_id=device, device_id_type=MESH)

    each(1, 32, lambda d: greet((lax.rem(me + d, 32), my_orb)))
    each(1, 16, lambda d: greet(stack(lax.rem(zc + d, 16))[0]))

    def remote(src, dst, send_sem, recv_sem, device):
        return pltpu.make_async_remote_copy(src_ref=src, dst_ref=dst, send_sem=send_sem, recv_sem=recv_sem,
                                            device_id=device, device_id_type=MESH)

    def pot_copy(d):
        half = pl.ds(2 * core, 2)
        remote(pot_ref.at[half], pot5.at[me, core], psend, precv, (lax.rem(me + 9 * d, 32), my_orb)).start()

    def orb_copy(k, d):
        to = lax.rem(me + 9 * d, 32)
        remote(orb_ref.at[2 * to + k], a.at[k, pl.ds(4 + 4 * me, 4)], send.at[k], recv.at[k], (to, my_orb)).start()

    pot_own = pltpu.make_async_copy(pot_ref.at[pl.ds(2 * core, 2)], pot5.at[me, core], own.at[2])
    pot_own.start()
    local = [pltpu.make_async_copy(orb_ref.at[2 * me + k], a.at[k, pl.ds(4 + 4 * me, 4)], own.at[k]) for k in range(2)]
    for copy in local:
        copy.start()
    pl.semaphore_wait(bar, 46)
    each(1, 32, pot_copy)
    each(1, 32, lambda d: orb_copy(0, d))
    each(1, 32, lambda d: orb_copy(1, d))
    pot_own.wait()
    wait_bytes(pot5.at[pl.ds(0, 31), 0], precv)
    pot_swap = remote(pot5.at[:, core], pot5.at[:, core], esend.at[2], erecv.at[2], partner)
    pot_swap.start()
    for copy in local:
        copy.wait()
    along_z = shift_matrix()

    lows = (1 - z_lo, z_lo)

    def plane_copy(k, s, d):
        to = lax.rem(xy + 5 * d, 16)
        planes = pl.ds(4 * lows[s], 4)
        remote(c.at[k, pl.ds(8 * to + 4 * lows[s], 4)], slab.at[k, xy, planes],
               asend.at[k, s], arecv.at[k, s], plane(to)).start()

    def cell_copy(k, s, d):
        to = lax.rem(my_orb + 3 * d, 8)
        remote(slab.at[k, :, 4 * lows[s] + to // 2, lax.rem(to, 2)], m6.at[my_orb, :, z_lo, k],
               bsend.at[k], brecv.at[k], (xy * 2 + lows[s], to)).start()

    for k in range(2):
        wait_bytes(a.at[k, pl.ds(0, 124)], recv.at[k])
        if k == 0:
            pot_swap.wait()
        ak, bk, ck = a.at[k], b.at[k], c.at[k]

        def put_b(base, value):
            bk[pl.ds(base + 4, STEP)] = value

        def put_a(base, value):
            ak[pl.ds(base + 4, STEP)] = value

        def put_c(base, value):
            ck[pl.ds(base, STEP), 0] = value[:, 0:4]
            ck[pl.ds(base, STEP), 1] = value[:, 4:8]

        fill(ak)
        apply_level(ak, pot, along_z, 0.25, None, put_b)
        fill(bk)
        apply_level(bk, pot, along_z, 0.5, ak, put_a)
        fill(ak)
        apply_level(ak, pot, along_z, 0.5, bk, put_c)
        for s in range(2):
            each(1, 16, lambda d: plane_copy(k, s, d))
        mine = pltpu.make_async_copy(c.at[k, pl.ds(8 * xy, 8)], slab.at[k, xy], own.at[3 + k])
        mine.start()
        mine.wait()
    for k in range(2):
        for s in range(2):
            wait_bytes(slab.at[k, pl.ds(0, 15), pl.ds(0, 4)], arecv.at[k, s])
            each(s, 8, lambda d: cell_copy(k, s, d))
        mine = pltpu.make_async_copy(slab.at[k, :, 4 * z_lo + z_hi, core], m6.at[my_orb, :, z_lo, k], own.at[5 + k])
        mine.start()
        mine.wait()
    for k in range(2):
        wait_bytes(slab.at[k, pl.ds(0, 15)], brecv.at[k])

    f_ref = m6.reshape(512, 4, 128)
    for q in range(4):
        x_ref[:, 128 * q:128 * q + 128] = f_ref[:, q, :]

    def gram(j):
        xj = x_ref[128 * j:128 * j + 128, :]
        for i in range(j, 4):
            g_ref[blk(i, j), :] = dot(x_ref[128 * i:128 * i + 128, :], xj, NT)

    def half_rows(p, which):
        base, n = PIECES[p]
        return pl.ds(pl.multiple_of(base + 16 * n * which, 8), 16 * n)

    def own_rows(p, i):
        base, n = PIECES[p]
        return pl.ds(pl.multiple_of(base + 16 * n * core + n * i, 8), n)

    def box(p):
        return pl.ds(PIECES[p][0] // 2, 16 * PIECES[p][1])

    def core_copy(p):
        return remote(g_ref.at[half_rows(p, 1 - core)], cbuf.at[box(p)], csend.at[p], crecv.at[p], partner)

    def scatter(p, d):
        to = lax.rem(xy + 5 * d, 16)
        remote(g_ref.at[own_rows(p, to)], parts[p].at[xy], rsend.at[p], rrecv.at[p], plane(to)).start()

    def exchange(p, d):
        remote(zparts[p].at[z], zparts[p].at[z], zsend.at[p], zrecv.at[p], column(lax.rem(z + 3 * d, 8))).start()

    def gather(p, d):
        rows = a_ref.at[own_rows(p, xy)]
        remote(rows, rows, gsend.at[p], grecv.at[p], plane(lax.rem(xy + 5 * d, 16))).start()

    def core_swap(p):
        rows = a_ref.at[half_rows(p, core)]
        return remote(rows, rows, esend.at[p], erecv.at[p], partner)

    def start_scatter(p):
        core_copy(p).wait()
        rows = half_rows(p, core)
        g_ref[rows, :] = g_ref[rows, :] + cbuf[box(p), :]
        each(1, 16, lambda d: scatter(p, d))
        parts[p][xy] = g_ref[own_rows(p, xy), :]

    def start_exchange(p):
        wait_bytes(parts[p].at[pl.ds(0, 15)], rrecv.at[p])
        total = parts[p][0]
        for i in range(1, 16):
            total = total + parts[p][i]
        zparts[p][z] = total
        each(1, 8, lambda d: exchange(p, d))

    def start_gather(p):
        wait_bytes(zparts[p].at[pl.ds(0, 7)], zrecv.at[p])
        total = zparts[p][0]
        for i in range(1, 8):
            total = total + zparts[p][i]
        a_ref[own_rows(p, xy), :] = total * (1.0 / CELLS)
        each(1, 16, lambda d: gather(p, d))

    def start_swap(p):
        wait_bytes(parts[p].at[pl.ds(0, 15)], grecv.at[p])
        wait_bytes(parts[p].at[pl.ds(0, 15)], gsend.at[p])
        core_swap(p).start()

    gram(0)
    core_copy(0).start()
    for j in range(1, 4):
        gram(j)
    core_copy(1).start()
    for stage in (start_scatter, start_exchange, start_gather, start_swap):
        for p in range(2):
            stage(p)
    core_swap(0).wait()

    def ends(to, first, count):
        rows = y_ref.at[pl.ds(64 * to + first, count)]
        return rows, out_ref.at[pl.ds(first, count), z_hi, core]

    def rotate_rows(b, start, count):
        to, first = 2 * b + start // 64, start % 64
        y = dot(w_ref[start:start + count, :], x_ref[128 * b:128 * b + 128, :], NN)
        for q in range(4):
            y_ref[128 * b + start:128 * b + start + count, q, :] = y[:, 128 * q:128 * q + 128]
        rows, place = ends(to, first, count)

        @pl.when(my_orb != to)
        def _():
            remote(rows, place, dsend, drecv, (me, to)).start()

        @pl.when(my_orb == to)
        def _():
            pltpu.make_async_copy(rows, place, own.at[7]).start()
        return y

    soon, later = [], []
    for b in range(4):
        tops = []

        def run(work):
            while work:
                work.pop(0)()

        count = 32 if b == 3 else 64
        after = {0: lambda: run(soon), 8: lambda: run(later)}
        for start in range(0, 128 - count, count):
            after[(start + count) // 8 - 1] = lambda start=start: tops.append(rotate_rows(b, start, count))
        factor_block(a_ref, w_ref, 128 * COLUMN[b], after)
        w = w_ref[...]
        if b == 0:
            core_swap(1).wait()
        low = {}

        def lower(i, b=b, w=w, low=low):
            low[i] = dot(a_ref[blk(i, b), :], w, NT)

        def update(i, j, low=low):
            a_ref[blk(i, j), :] = a_ref[blk(i, j), :] - dot(low[i], low[j], NT)

        if b < 3:
            lower(b + 1)
            update(b + 1, b + 1)
        tops.append(rotate_rows(b, 128 - count, count))
        y = jnp.concatenate(tops, axis=0) if b < 3 else None

        def solve(i, y=y, low=low):
            rows = slice(128 * i, 128 * i + 128)
            x_ref[rows, :] = x_ref[rows, :] - dot(low[i], y, NN)

        for i in range(b + 1, 4):
            if i > b + 1:
                later.append(functools.partial(lower, i))
                for j in range(b + 1, i + 1):
                    later.append(functools.partial(update, i, j))
            (later if i > b + 1 else soon).append(functools.partial(solve, i))

    wait_bytes(pot5.at[pl.ds(0, 31), 0], psend)
    for k in range(2):
        wait_bytes(a.at[k, pl.ds(0, 124)], send.at[k])
        for s in range(2):
            wait_bytes(slab.at[k, pl.ds(0, 15), pl.ds(0, 4)], asend.at[k, s])
        wait_bytes(slab.at[k, pl.ds(0, 15)], bsend.at[k])
    for p in range(2):
        wait_bytes(parts[p].at[pl.ds(0, 15)], rsend.at[p])
        wait_bytes(zparts[p].at[pl.ds(0, 7)], zsend.at[p])
    wait_bytes(y_ref.at[pl.ds(0, 64)], own.at[7])
    wait_bytes(y_ref.at[pl.ds(0, 448)], dsend)
    wait_bytes(y_ref.at[pl.ds(0, 448)], drecv)


def mega(orbitals, potential):
    dma, f32 = pltpu.SemaphoreType.DMA, jnp.float32

    def vmem(*shape):
        return pltpu.VMEM(shape, f32)

    return pl.pallas_call(
        mega_kernel,
        out_shape=jax.ShapeDtypeStruct((64, 4, 2, 4, 128), f32),
        in_specs=[any_spec()] * 2, out_specs=any_spec(),
        scratch_shapes=[vmem(2, 136, 8, 128), vmem(2, 136, 8, 128), vmem(32, 2, 2, 8, 128), vmem(2, 128, 2, 4, 128),
                        vmem(2, 16, 8, 2, 4, 128), vmem(8, 16, 2, 2, 4, 128),
                        vmem(512, 512), vmem(1280, 128), vmem(1280, 128), vmem(512, 4, 128), vmem(128, 128),
                        vmem(640, 128), vmem(16, 16, 128), vmem(16, 24, 128), vmem(8, 16, 128), vmem(8, 24, 128),
                        dma((2,)), dma((2,)), dma, dma, dma((2, 2)), dma((2, 2)), dma((2,)), dma((2,)), dma((8,)),
                        dma((2,)), dma((2,)), dma((2,)), dma((2,)), dma((2,)), dma((2,)),
                        dma((2,)), dma((2,)), dma((3,)), dma((3,)), dma, dma],
        compiler_params=pltpu.CompilerParams(collective_id=1, has_side_effects=True, vmem_limit_bytes=52 << 20),
    )(orbitals, potential)


def per_device(orbitals, potential):
    return mega(orbitals, potential).reshape(64, 4, 8, 128)


def solution(mesh):
    in_specs = (P("orb", "grid", None, None), P("grid", None, None))
    out_specs = P("orb", "grid", None, None)
    return jax.shard_map(
        per_device, mesh=mesh, in_specs=in_specs, out_specs=out_specs, check_vma=False
    )
```

```python
import functools
import jax, jax.numpy as jnp
from jax import lax
from jax.sharding import PartitionSpec as P
from jax.experimental import pallas as pl
from jax.experimental.pallas import tpu as pltpu
HI = lax.Precision.HIGHEST
NT = (((1,), (1,)), ((), ()))
NN = (((1,), (0,)), ((), ()))

def dot(a, b, dims):
    return lax.dot_general(a, b, dims, precision=HI, preferred_element_type=jnp.float32)

def row_of(block, j):
    return jnp.broadcast_to(block[j:j + 1, :], (8, 128))

def recip(d):
    r = pl.reciprocal(d, approx=True)
    return r * (2.0 - d * r)

def factor_block(s_ref, w_ref, base, after):
    sub = lax.broadcasted_iota(jnp.int32, (8, 128), 0)
    lane = lax.broadcasted_iota(jnp.int32, (8, 128), 1)
    s = [s_ref[pl.ds(base + 8 * i, 8), :] for i in range(16)]
    w = [jnp.where(lane == sub + 8 * i, 1.0, 0.0).astype(jnp.float32) for i in range(16)]
    for p in range(16):
        col = [jnp.broadcast_to(s[p][:, 8 * p + j:8 * p + j + 1], (8, 128)) for j in range(8)]
        fac, rinv, s_rows, w_rows = {}, [], [], []
        sp, wp = s[p], w[p]
        dvec = jnp.ones((8, 128), jnp.float32)
        first = col[0]
        for j in range(1, 8):
            first = jnp.where(sub == j, col[j], first)
        scale = pl.reciprocal(first, approx=True)

        def eliminate(j, d, r, below):
            nonlocal sp, wp, dvec
            rinv.append(r)
            dvec = jnp.where(sub == j, d, dvec)
            m = below * r
            for k in range(j + 1, 8):
                fac[j, k] = row_of(col[k], j)
                col[k] = col[k] - m * fac[j, k]
            s_rows.append(row_of(sp, j))
            w_rows.append(row_of(wp, j))
            if j < 7:
                sp = sp - m * s_rows[j]
                wp = wp - m * w_rows[j]

        for j in range(0, 8, 2):
            d0, off, d1 = row_of(col[j], j), row_of(col[j + 1], j), row_of(col[j + 1], j + 1)
            k0 = row_of(scale, j)
            d0k = d0 * k0
            both = d0k * d1 - (off * k0) * off
            r0, rb = recip(d0), recip(both)
            eliminate(j, d0, r0, jnp.where(sub > j, col[j], 0.0))
            eliminate(j + 1, both / d0k, d0k * rb, jnp.where(sub > j + 1, col[j + 1], 0.0))
        w_ref[8 * p:8 * p + 8, :] = wp * lax.rsqrt(dvec)
        for i in range(p + 1, 16):
            raw = [jnp.broadcast_to(s[i][:, 8 * p + j:8 * p + j + 1], (8, 128)) for j in range(8)]
            si, wi = s[i], w[i]
            for j in range(8):
                m = raw[j] * rinv[j]
                for k in range(j + 1, 8):
                    raw[k] = raw[k] - m * fac[j, k]
                si = si - m * s_rows[j]
                wi = wi - m * w_rows[j]
            s[i], w[i] = si, wi
        if p in after:
            after[p]()

W = (-205.0 / 72.0, 8.0 / 5.0, -1.0 / 5.0, 8.0 / 315.0, -1.0 / 560.0)

MESH = pl.DeviceIdType.MESH


def any_spec():
    return pl.BlockSpec(memory_space=pl.ANY)


STEP = 64


def shift_matrix():
    i = lax.broadcasted_iota(jnp.int32, (128, 128), 0)
    j = lax.broadcasted_iota(jnp.int32, (128, 128), 1)
    apart = jnp.abs(i - j)
    apart = jnp.minimum(apart, 128 - apart)
    out = jnp.zeros((128, 128), jnp.float32)
    for m in range(1, 5):
        out = jnp.where(apart == m, W[m], out)
    return out


def apply_level(src, pot_ref, along_z, gain, prev, put):
    w = [-0.5 * gain * c for c in W]
    shifts = along_z * (-0.5 * gain)

    def body(t, carry):
        base = t * STEP
        win = src[pl.ds(base, STEP + 8)]
        v = win[4:4 + STEP]
        acc = (gain * (pot_ref[pl.ds(base, STEP)] - 7.0) + 3.0 * w[0]) * v
        acc = acc + dot(v.reshape(STEP * 8, 128), shifts, NN).reshape(STEP, 8, 128)
        u1 = pltpu.roll(v, 1, 1) + pltpu.roll(v, 7, 1)
        r4 = pltpu.roll(v, 4, 1)
        side = [u1, pltpu.roll(v + r4, 2, 1), pltpu.roll(u1, 4, 1), r4 + r4]
        for m in range(1, 5):
            xx = win[4 + m:4 + m + STEP] + win[4 - m:4 - m + STEP]
            acc = acc + w[m] * (side[m - 1] + xx)
        if prev is not None:
            acc = acc - prev[pl.ds(base + 4, STEP)]
        put(base, acc)
        return carry

    lax.fori_loop(0, 128 // STEP, body, 0)


def fill(ref):
    ref[0:4] = ref[128:132]
    ref[132:136] = ref[4:8]


COLUMN = (0, 4, 7, 9)
PIECES = ((0, 40),)
CELLS = 128.0 * 8.0 * 128.0


def blk(i, j):
    return pl.ds(128 * (COLUMN[j] + i - j), 128)


def each(first, last, do):
    def body(d, carry):
        do(d)
        return carry
    lax.fori_loop(first, last, body, 0, unroll=True)


def wait_bytes(like, sem):
    pltpu.make_async_copy(like, like, sem).wait()


def mega_kernel(orb_ref, pot_ref, out_ref, a, b, pot5, c, slab, m6, x_ref, g_ref, a_ref, y_ref, w_ref, cbuf,
                parts0, zparts0, send, recv, psend, precv, asend, arecv, bsend, brecv, own,
                csend, crecv, rsend, rrecv, zsend, zrecv, gsend, grecv, esend, erecv, dsend, drecv):
    me, my_orb = lax.axis_index("grid"), lax.axis_index("orb")
    xy, z_lo = me // 2, lax.rem(me, 2)
    z_hi, core = my_orb // 2, lax.rem(my_orb, 2)
    z = z_hi * 2 + z_lo
    zc = z * 2 + core
    pot = pot5.reshape(128, 8, 128)
    parts, zparts = (parts0,), (zparts0,)
    partner = (me, z_hi * 2 + 1 - core)

    def stack(i):
        at, k = i // 2, lax.rem(i, 2)
        lo, hi = lax.rem(at, 2), at // 2
        return (xy * 2 + lo, hi * 2 + k), lo, hi, k

    def plane(i):
        return (i * 2 + z_lo, my_orb)

    def column(i):
        return (xy * 2 + lax.rem(i, 2), (i // 2) * 2 + core)

    bar = pltpu.get_barrier_semaphore()

    def greet(device):
        pl.semaphore_signal(bar, inc=1, device_id=device, device_id_type=MESH)

    each(1, 32, lambda d: greet((lax.rem(me + d, 32), my_orb)))
    each(1, 16, lambda d: greet(stack(lax.rem(zc + d, 16))[0]))

    def remote(src, dst, send_sem, recv_sem, device):
        return pltpu.make_async_remote_copy(src_ref=src, dst_ref=dst, send_sem=send_sem, recv_sem=recv_sem,
                                            device_id=device, device_id_type=MESH)

    def pot_copy(d):
        half = pl.ds(2 * core, 2)
        remote(pot_ref.at[half], pot5.at[me, core], psend, precv, (lax.rem(me + 9 * d, 32), my_orb)).start()

    def orb_copy(k, d):
        to = lax.rem(me + 9 * d, 32)
        remote(orb_ref.at[2 * to + k], a.at[k, pl.ds(4 + 4 * me, 4)], send.at[k], recv.at[k], (to, my_orb)).start()

    pot_own = pltpu.make_async_copy(pot_ref.at[pl.ds(2 * core, 2)], pot5.at[me, core], own.at[2])
    pot_own.start()
    local = [pltpu.make_async_copy(orb_ref.at[2 * me + k], a.at[k, pl.ds(4 + 4 * me, 4)], own.at[k]) for k in range(2)]
    for copy in local:
        copy.start()
    pl.semaphore_wait(bar, 46)
    each(1, 32, pot_copy)
    each(1, 32, lambda d: orb_copy(0, d))
    each(1, 32, lambda d: orb_copy(1, d))
    pot_own.wait()
    wait_bytes(pot5.at[pl.ds(0, 31), 0], precv)
    pot_swap = remote(pot5.at[:, core], pot5.at[:, core], esend.at[2], erecv.at[2], partner)
    pot_swap.start()
    for copy in local:
        copy.wait()
    along_z = shift_matrix()

    lows = (1 - z_lo, z_lo)

    def plane_copy(k, s, d):
        to = lax.rem(xy + 5 * d, 16)
        planes = pl.ds(4 * lows[s], 4)
        remote(c.at[k, pl.ds(8 * to + 4 * lows[s], 4)], slab.at[k, xy, planes],
               asend.at[k, s], arecv.at[k, s], plane(to)).start()

    def cell_copy(k, s, d):
        to = lax.rem(my_orb + 3 * d, 8)
        remote(slab.at[k, :, 4 * lows[s] + to // 2, lax.rem(to, 2)], m6.at[my_orb, :, z_lo, k],
               bsend.at[k], brecv.at[k], (xy * 2 + lows[s], to)).start()

    for k in range(2):
        wait_bytes(a.at[k, pl.ds(0, 124)], recv.at[k])
        if k == 0:
            pot_swap.wait()
        ak, bk, ck = a.at[k], b.at[k], c.at[k]

        def put_b(base, value):
            bk[pl.ds(base + 4, STEP)] = value

        def put_a(base, value):
            ak[pl.ds(base + 4, STEP)] = value

        def put_c(base, value):
            ck[pl.ds(base, STEP), 0] = value[:, 0:4]
            ck[pl.ds(base, STEP), 1] = value[:, 4:8]

        fill(ak)
        apply_level(ak, pot, along_z, 0.25, None, put_b)
        fill(bk)
        apply_level(bk, pot, along_z, 0.5, ak, put_a)
        fill(ak)
        apply_level(ak, pot, along_z, 0.5, bk, put_c)
        for s in range(2):
            each(1, 16, lambda d: plane_copy(k, s, d))
        mine = pltpu.make_async_copy(c.at[k, pl.ds(8 * xy, 8)], slab.at[k, xy], own.at[3 + k])
        mine.start()
        mine.wait()
    for k in range(2):
        for s in range(2):
            wait_bytes(slab.at[k, pl.ds(0, 15), pl.ds(0, 4)], arecv.at[k, s])
            each(s, 8, lambda d: cell_copy(k, s, d))
        mine = pltpu.make_async_copy(slab.at[k, :, 4 * z_lo + z_hi, core], m6.at[my_orb, :, z_lo, k], own.at[5 + k])
        mine.start()
        mine.wait()
    for k in range(2):
        wait_bytes(slab.at[k, pl.ds(0, 15)], brecv.at[k])

    f_ref = m6.reshape(512, 4, 128)
    for q in range(4):
        x_ref[:, 128 * q:128 * q + 128] = f_ref[:, q, :]

    def gram(j):
        xj = x_ref[128 * j:128 * j + 128, :]
        for i in range(j, 4):
            g_ref[blk(i, j), :] = dot(x_ref[128 * i:128 * i + 128, :], xj, NT)

    def half_rows(p, which):
        base, n = PIECES[p]
        return pl.ds(pl.multiple_of(base + 16 * n * which, 8), 16 * n)

    def own_rows(p, i):
        base, n = PIECES[p]
        return pl.ds(pl.multiple_of(base + 16 * n * core + n * i, 8), n)

    def box(p):
        return pl.ds(PIECES[p][0] // 2, 16 * PIECES[p][1])

    def core_copy(p):
        return remote(g_ref.at[half_rows(p, 1 - core)], cbuf.at[box(p)], csend.at[p], crecv.at[p], partner)

    def scatter(p, d):
        to = lax.rem(xy + 5 * d, 16)
        remote(g_ref.at[own_rows(p, to)], parts[p].at[xy], rsend.at[p], rrecv.at[p], plane(to)).start()

    def exchange(p, d):
        remote(zparts[p].at[z], zparts[p].at[z], zsend.at[p], zrecv.at[p], column(lax.rem(z + 3 * d, 8))).start()

    def gather(p, d):
        rows = a_ref.at[own_rows(p, xy)]
        remote(rows, rows, gsend.at[p], grecv.at[p], plane(lax.rem(xy + 5 * d, 16))).start()

    def core_swap(p):
        rows = a_ref.at[half_rows(p, core)]
        return remote(rows, rows, esend.at[p], erecv.at[p], partner)

    def start_scatter(p):
        core_copy(p).wait()
        rows = half_rows(p, core)
        g_ref[rows, :] = g_ref[rows, :] + cbuf[box(p), :]
        each(1, 16, lambda d: scatter(p, d))
        parts[p][xy] = g_ref[own_rows(p, xy), :]

    def start_exchange(p):
        wait_bytes(parts[p].at[pl.ds(0, 15)], rrecv.at[p])
        total = parts[p][0]
        for i in range(1, 16):
            total = total + parts[p][i]
        zparts[p][z] = total
        each(1, 8, lambda d: exchange(p, d))

    def start_gather(p):
        wait_bytes(zparts[p].at[pl.ds(0, 7)], zrecv.at[p])
        total = zparts[p][0]
        for i in range(1, 8):
            total = total + zparts[p][i]
        a_ref[own_rows(p, xy), :] = total * (1.0 / CELLS)
        each(1, 16, lambda d: gather(p, d))

    def start_swap(p):
        wait_bytes(parts[p].at[pl.ds(0, 15)], grecv.at[p])
        wait_bytes(parts[p].at[pl.ds(0, 15)], gsend.at[p])
        core_swap(p).start()

    for j in range(4):
        gram(j)
    core_copy(0).start()
    for stage in (start_scatter, start_exchange, start_gather, start_swap):
        stage(0)
    core_swap(0).wait()

    def ends(to, first, count):
        rows = y_ref.at[pl.ds(64 * to + first, count)]
        return rows, out_ref.at[pl.ds(first, count), z_hi, core]

    def rotate_rows(b, start, count):
        to, first = 2 * b + start // 64, start % 64
        y = dot(w_ref[start:start + count, :], x_ref[128 * b:128 * b + 128, :], NN)
        for q in range(4):
            y_ref[128 * b + start:128 * b + start + count, q, :] = y[:, 128 * q:128 * q + 128]
        rows, place = ends(to, first, count)

        @pl.when(my_orb != to)
        def _():
            remote(rows, place, dsend, drecv, (me, to)).start()

        @pl.when(my_orb == to)
        def _():
            pltpu.make_async_copy(rows, place, own.at[7]).start()
        return y

    soon, later = [], []
    for b in range(4):
        tops = []

        def run(work):
            while work:
                work.pop(0)()

        count = 32 if b == 3 else 64
        after = {0: lambda: run(soon), 8: lambda: run(later)}
        for start in range(0, 128 - count, count):
            after[(start + count) // 8 - 1] = lambda start=start: tops.append(rotate_rows(b, start, count))
        factor_block(a_ref, w_ref, 128 * COLUMN[b], after)
        w = w_ref[...]
        low = {}

        def lower(i, b=b, w=w, low=low):
            low[i] = dot(a_ref[blk(i, b), :], w, NT)

        def update(i, j, low=low):
            a_ref[blk(i, j), :] = a_ref[blk(i, j), :] - dot(low[i], low[j], NT)

        if b < 3:
            lower(b + 1)
            update(b + 1, b + 1)
        tops.append(rotate_rows(b, 128 - count, count))
        y = jnp.concatenate(tops, axis=0) if b < 3 else None

        def solve(i, y=y, low=low):
            rows = slice(128 * i, 128 * i + 128)
            x_ref[rows, :] = x_ref[rows, :] - dot(low[i], y, NN)

        for i in range(b + 1, 4):
            if i > b + 1:
                later.append(functools.partial(lower, i))
                for j in range(b + 1, i + 1):
                    later.append(functools.partial(update, i, j))
            (later if i > b + 1 else soon).append(functools.partial(solve, i))

    wait_bytes(pot5.at[pl.ds(0, 31), 0], psend)
    for k in range(2):
        wait_bytes(a.at[k, pl.ds(0, 124)], send.at[k])
        for s in range(2):
            wait_bytes(slab.at[k, pl.ds(0, 15), pl.ds(0, 4)], asend.at[k, s])
        wait_bytes(slab.at[k, pl.ds(0, 15)], bsend.at[k])
    for p in range(1):
        wait_bytes(parts[p].at[pl.ds(0, 15)], rsend.at[p])
        wait_bytes(zparts[p].at[pl.ds(0, 7)], zsend.at[p])
    wait_bytes(y_ref.at[pl.ds(0, 64)], own.at[7])
    wait_bytes(y_ref.at[pl.ds(0, 448)], dsend)
    wait_bytes(y_ref.at[pl.ds(0, 448)], drecv)


def mega(orbitals, potential):
    dma, f32 = pltpu.SemaphoreType.DMA, jnp.float32

    def vmem(*shape):
        return pltpu.VMEM(shape, f32)

    return pl.pallas_call(
        mega_kernel,
        out_shape=jax.ShapeDtypeStruct((64, 4, 2, 4, 128), f32),
        in_specs=[any_spec()] * 2, out_specs=any_spec(),
        scratch_shapes=[vmem(2, 136, 8, 128), vmem(2, 136, 8, 128), vmem(32, 2, 2, 8, 128), vmem(2, 128, 2, 4, 128),
                        vmem(2, 16, 8, 2, 4, 128), vmem(8, 16, 2, 2, 4, 128),
                        vmem(512, 512), vmem(1280, 128), vmem(1280, 128), vmem(512, 4, 128), vmem(128, 128),
                        vmem(640, 128), vmem(16, 40, 128), vmem(8, 40, 128),
                        dma((2,)), dma((2,)), dma, dma, dma((2, 2)), dma((2, 2)), dma((2,)), dma((2,)), dma((8,)),
                        dma((2,)), dma((2,)), dma((2,)), dma((2,)), dma((2,)), dma((2,)),
                        dma((2,)), dma((2,)), dma((3,)), dma((3,)), dma, dma],
        compiler_params=pltpu.CompilerParams(collective_id=1, has_side_effects=True, vmem_limit_bytes=52 << 20),
    )(orbitals, potential)


def per_device(orbitals, potential):
    return mega(orbitals, potential).reshape(64, 4, 8, 128)


def solution(mesh):
    in_specs = (P("orb", "grid", None, None), P("grid", None, None))
    out_specs = P("orb", "grid", None, None)
    return jax.shard_map(
        per_device, mesh=mesh, in_specs=in_specs, out_specs=out_specs, check_vma=False
    )
```
